32 devices in a mesh: lon: 16 (over z, x, core), lat: 2 (over y).
Axes of the slice: x: 2, y: 2, z: 4, core: 2. Of those that a mesh axis runs over, the one named last changes fastest.
Arguments:
- earlier_state: float32 [4, 4, 128, 8192], P(None, None, 'lat', 'lon'), may hold values from -6 to 6
- present_state: float32 [4, 4, 128, 8192], P(None, None, 'lat', 'lon'), may hold values from -6 to 6
- scalar_wet_flags: int32 [4, 128, 8192], P(None, 'lat', 'lon'), may hold values 0 or 1
- eastside_wet_flags: int32 [4, 128, 8192], P(None, 'lat', 'lon'), may hold values 0 or 1
- northside_wet_flags: int32 [4, 128, 8192], P(None, 'lat', 'lon'), may hold values 0 or 1
Outputs:
- after: float32 [4, 4, 128, 8192], P(None, None, 'lat', 'lon')
- filtered: float32 [4, 4, 128, 8192], P(None, None, 'lat', 'lon')
The draws below stay inside these ranges and needn't reach their ends.
All inputs are finite; a program needn't handle non-finite values. No bound on the sum of `scalar_wet_flags` or of `eastside_wet_flags` or of `northside_wet_flags` on one device may be relied on, other than what follows from the above.
Results may differ from the reference program's by a relative error of at most 0.00002.
Values sent between devices are 32-bit elements; how exact they have to be, the bound alone decides.
No kernel may reach another device: no remote copies, remote signals or barrier semaphores. Data moves between devices by JAX's collectives and lax.ppermute only.
A program may use at most 128 MiB of HBM per device.

```python
import jax
import jax.numpy as jnp
from jax import lax

VERTICAL_LAYERS = 4
WEST_EAST_SPAN = 8192
SOUTH_NORTH_SPAN = 128


def place_ends(result, own_key, least, high):
    extent = result.shape
    place = [jax.random.randint(jax.random.fold_in(own_key, axis), (), 0, extent[axis]) for axis in range(len(extent))]
    result = result.at[tuple(place)].set(least)
    longest = extent.index(max(extent))
    place[longest] = (place[longest] + 1) % extent[longest]
    return result.at[tuple(place)].set(high)


def steps_of(rng, shape, shards, smallest, largest):
    level = 1.0
    for dim, blocks in shards:
        draws = jax.random.uniform(jax.random.fold_in(jax.random.fold_in(rng, 6), dim), (blocks,), jnp.float32, smallest / len(shards), largest / len(shards))
        level = level * jnp.repeat(jnp.exp(draws), shape[dim] // blocks).reshape((-1,) + (1,) * (len(shape) - 1 - dim))
    return level


def gaussian(own_key, dims, scale, reach, split=(), kind=jnp.bfloat16):
    drawn = scale * jax.random.normal(own_key, dims, jnp.float32)
    if split:
        drawn = drawn * steps_of(own_key, dims, split, -0.22, 0.18)
    return jnp.clip(drawn, -reach, reach).astype(kind)


def setup_inputs(seed: int = 0) -> dict:
    streams_of = jax.random.split(jax.random.key(seed), 6)
    earlier_state = gaussian(streams_of[0], (4, VERTICAL_LAYERS, SOUTH_NORTH_SPAN, WEST_EAST_SPAN), 1.0, 6.0, ((2, 2), (3, 16)), jnp.float32)
    present_state = gaussian(streams_of[1], (4, VERTICAL_LAYERS, SOUTH_NORTH_SPAN, WEST_EAST_SPAN), 1.0, 6.0, ((2, 2), (3, 16)), jnp.float32)
    scalar_wet_flags = place_ends((jax.random.randint(streams_of[2], (VERTICAL_LAYERS, SOUTH_NORTH_SPAN, WEST_EAST_SPAN), 0, 5) < 4).astype(jnp.int32), jax.random.fold_in(streams_of[2], 1), 0, 1)
    eastside_wet_flags = place_ends((jax.random.randint(streams_of[3], (VERTICAL_LAYERS, SOUTH_NORTH_SPAN, WEST_EAST_SPAN), 0, 5) < 4).astype(jnp.int32), jax.random.fold_in(streams_of[3], 1), 0, 1)
    northside_wet_flags = place_ends((jax.random.randint(streams_of[4], (VERTICAL_LAYERS, SOUTH_NORTH_SPAN, WEST_EAST_SPAN), 0, 5) < 4).astype(jnp.int32), jax.random.fold_in(streams_of[4], 1), 0, 1)
    return {"earlier_state": earlier_state, "present_state": present_state, "scalar_wet_flags": scalar_wet_flags, "eastside_wet_flags": eastside_wet_flags, "northside_wet_flags": northside_wet_flags}


advect_coef = 0.5
diffuse_coef = 0.25
twice_step = 0.5
gravity = 0.5
coriolis = 0.5
thermal = 0.2
haline = 0.15
asselin = 0.1


def pressure(temp, salt):
    density = haline * salt - thermal * temp
    return jnp.cumsum(density, axis=0) - 0.5 * density


def face_flux(here, ahead, speed, face_mask):
    return advect_coef * speed * (here[:4] + ahead[:4]) * 0.5 - diffuse_coef * face_mask * (ahead[4:] - here[4:])


def level_step(items):
    prior, current, tracer_cell_mask, mask_u, southnorth_wet_flags, pres = items
    fmask = jnp.stack([tracer_cell_mask, tracer_cell_mask, mask_u, southnorth_wet_flags])
    curm = current * fmask
    befm = prior * fmask
    both = jnp.concatenate([curm, befm], 0)
    signs = jnp.array([1.0, 1.0, -1.0, -1.0, 1.0, 1.0, -1.0, -1.0], jnp.float32)[:, None]
    ghost = both[:, -1, ::-1] * signs
    east = jnp.roll(both, -1, -1)
    north = jnp.concatenate([both[:, 1:, :], ghost[:, None, :]], 1)
    flux_e = face_flux(both, east, curm[2], mask_u)
    northern_face_flux = face_flux(both, north, curm[3], southnorth_wet_flags)
    flux_w = jnp.roll(flux_e, 1, -1)
    flux_s = jnp.concatenate([jnp.zeros_like(northern_face_flux[:, :1, :]), northern_face_flux[:, :-1, :]], 1)
    pres_e = jnp.roll(pres, -1, -1)
    pres_n = jnp.concatenate([pres[1:, :], pres[-1:, ::-1]], 0)
    rows = jnp.arange(SOUTH_NORTH_SPAN, dtype=jnp.float32)
    cor = (coriolis * (2.0 * (rows + 0.5) / SOUTH_NORTH_SPAN - 1.0))[:, None]
    tend = -((flux_e - flux_w) + (northern_face_flux - flux_s))
    zonal_velocity_tendency = tend[2] + (cor * curm[3] - gravity * mask_u * (pres_e - pres))
    tend_v = tend[3] - (cor * curm[2] + gravity * southnorth_wet_flags * (pres_n - pres))
    tend = jnp.stack([tend[0], tend[1], zonal_velocity_tendency, tend_v])
    after = (befm + twice_step * tend) * fmask
    filtered = curm + asselin * (befm - 2.0 * curm + after)
    return after, filtered


def reference(earlier_state, present_state, scalar_wet_flags, eastside_wet_flags, northside_wet_flags):
    tracer_cell_mask = scalar_wet_flags.astype(jnp.float32)
    mask_u = eastside_wet_flags.astype(jnp.float32)
    southnorth_wet_flags = northside_wet_flags.astype(jnp.float32)
    pres = pressure(present_state[0] * tracer_cell_mask, present_state[1] * tracer_cell_mask)
    after, filtered = lax.map(level_step, (jnp.moveaxis(earlier_state, 1, 0), jnp.moveaxis(present_state, 1, 0), tracer_cell_mask, mask_u, southnorth_wet_flags, pres))
    return jnp.moveaxis(after, 0, 1), jnp.moveaxis(filtered, 0, 1)
```

```python
import functools

import jax
import jax.numpy as jnp
from jax import lax
from jax.experimental import pallas as pl
from jax.experimental.pallas import tpu as pltpu
from jax.sharding import PartitionSpec as P

advect_coef = 0.5
diffuse_coef = 0.25
twice_step = 0.5
gravity = 0.5
coriolis = 0.5
thermal = 0.2
haline = 0.15
asselin = 0.1

LANES = 128
SUBS = 8
FIELDS = 4
LEVELS = 4
ROWS = FIELDS * LEVELS
VMEM_LIMIT = 24 * 1024 * 1024

speed_coef = advect_coef * 0.5
ANY = pl.BlockSpec(memory_space=pl.ANY)
VMEM = pl.BlockSpec(memory_space=pltpu.VMEM)


def mask_of(field):
    return max(field - 1, 0)


def lane_ids(shape):
    return lax.broadcasted_iota(jnp.int32, shape, len(shape) - 1)


def row_ids(shape):
    return lax.broadcasted_iota(jnp.int32, shape, len(shape) - 2)


def halved(x):
    half = x.shape[0] // 2
    return jnp.where(lane_ids((half, LANES)) < LANES // 2, x[:half], pltpu.roll(x[half:], LANES // 2, 1))


def edges_kernel(
    n_lat,
    earlier, present, scalar_flags, east_flags, north_flags,
    pay_a, pay_b, pay_west, pay_east, coef_north, coef_south, coef_west, coef_east,
    col_state, col_flag, row_state, row_flag, sems,
):
    height, width = present.shape[2], present.shape[3]
    lat = lax.axis_index("lat")
    flags = (scalar_flags, east_flags, north_flags)
    copies = []
    for side in range(2):
        rows = pl.ds(0 if side == 0 else height - SUBS, SUBS)
        for t, state in enumerate((present, earlier)):
            copies.append((state.at[:, :, rows, :], row_state.at[side, t]))
        for t, flag in enumerate(flags):
            copies.append((flag.at[:, rows, :], row_flag.at[side, t]))
    for side in range(2):
        cols = pl.ds(0 if side == 0 else width - LANES, LANES)
        for t, state in enumerate((present, earlier)):
            copies.append((state.at[:, :, :, cols], col_state.at[side, t]))
        for t, flag in enumerate(flags):
            copies.append((flag.at[:, :, cols], col_flag.at[side, t]))
    copies = [
        pltpu.make_async_copy(src, dst, sems.at[i]) for i, (src, dst) in enumerate(copies)
    ]
    for copy in copies:
        copy.start()
    for copy in copies[:10]:
        copy.wait()

    sub = row_ids((SUBS, LANES))
    n_tiles = width // LANES

    def row_pack(side, at, j):
        line = pl.ds(at, 1)
        cols = pl.ds(j * LANES, LANES)

        def gather(rows):
            packed = jnp.broadcast_to(rows[0], (SUBS, LANES))
            for k in range(1, SUBS):
                packed = jnp.where(sub == k, jnp.broadcast_to(rows[k], (SUBS, LANES)), packed)
            return packed

        def flag_row(t, l):
            return row_flag[side, t, l, line, cols].astype(jnp.float32)

        fm = [
            gather([flag_row(mask_of(f), l) for f in (2 * h, 2 * h + 1) for l in range(LEVELS)])
            for h in range(2)
        ]
        cur, bef = (
            [
                fm[h]
                * gather([row_state[side, t, f, l, line, cols] for f in (2 * h, 2 * h + 1) for l in range(LEVELS)])
                for h in range(2)
            ]
            for t in range(2)
        )
        return fm, cur, bef

    lane = lane_ids((SUBS, LANES))
    back = LANES - 1 - lane
    even = lat % 2 == 0
    is_top = lat == n_lat - 1
    for j in range(n_tiles):
        cols = pl.ds(j * LANES, LANES)
        fm, cur, bef = row_pack(1, SUBS - 1, j)
        low_v = pltpu.roll(cur[1], 4, 0)
        s = speed_coef * jnp.where(sub < 4, low_v, cur[1])
        m = diffuse_coef * jnp.where(sub < 4, pltpu.roll(fm[1], 4, 0), fm[1])
        g = [s * cur[h] + m * bef[h] for h in range(2)]
        for h in range(2):
            at = pl.ds(h * SUBS, SUBS)
            coef_north[at, cols] = -twice_step * fm[h] * s
            coef_north[pl.ds(ROWS + h * SUBS, SUBS), cols] = twice_step * fm[h] * m
        coef_north[pl.ds(2 * ROWS, SUBS), cols] = jnp.where(sub < 4, 0.0, -twice_step * gravity * fm[1])

        fm_s, cur_s, bef_s = row_pack(0, 0, j)
        for h in range(2):
            at = pl.ds(h * SUBS, SUBS)
            coef_south[at, cols] = twice_step * fm_s[h]
            coef_south[pl.ds(ROWS + h * SUBS, SUBS), cols] = twice_step * cur_s[h]
            coef_south[pl.ds(2 * ROWS + h * SUBS, SUBS), cols] = -twice_step * bef_s[h]

        north_going = g + [s, m]
        south_going = cur_s + bef_s
        for q in range(4):
            at = pl.ds(q * SUBS, SUBS)
            pay_a[at, cols] = jnp.where(even, north_going[q], south_going[q])

        @pl.when(jnp.logical_not(is_top))
        def _():
            for q in range(4):
                below = jnp.where(lat == 0, 0.0, south_going[q])
                pay_b[pl.ds((4 * j + q) * SUBS, SUBS), :] = jnp.where(even, below, north_going[q])

        @pl.when(is_top)
        def _():
            for q, x in enumerate(cur + bef):
                mirrored = pl.ds((4 * (n_tiles - 1 - j) + q) * SUBS, SUBS)
                turned = jnp.take_along_axis(x, back, axis=1)
                pay_b[mirrored, :] = turned if q % 2 == 0 else -turned

    for copy in copies[10:]:
        copy.wait()

    lane = lane_ids((height, LANES))
    def col_pack(side, at):
        def column(x):
            return jnp.broadcast_to(x[:, at : at + 1], (height, LANES))

        def flag_col(t, l):
            return column(col_flag[side, t, l, :, :].astype(jnp.float32))

        masks = [[flag_col(t, l) for l in range(LEVELS)] for t in range(3)]
        base = lane & 15
        fm = masks[2][LEVELS - 1]
        for f in range(FIELDS):
            for l in range(LEVELS):
                if f * LEVELS + l < ROWS - 1:
                    fm = jnp.where(base == f * LEVELS + l, masks[mask_of(f)][l], fm)
        both = jnp.zeros((height, LANES), jnp.float32)
        u = []
        for t in range(2):
            for f in range(FIELDS):
                for l in range(LEVELS):
                    x = column(col_state[side, t, f, l, :, :])
                    if t == 0 and f == 2:
                        u.append(x)
                    both = jnp.where(lane == t * ROWS + f * LEVELS + l, x, both)
        return masks[1], fm, both * fm, u

    level = lane & 3
    _, fm, both, _ = col_pack(0, 0)
    rho = jnp.where(lane < LEVELS, haline * pltpu.roll(both, LANES - LEVELS, 1) - thermal * both, 0.0)
    total = rho + pltpu.roll(rho, 1, 1)
    total = total + pltpu.roll(total, 2, 1)
    pres = jnp.where(lane < LEVELS, total - 0.5 * rho, 0.0)
    going_west = both + pltpu.roll(pres, 2 * ROWS + 2 * LEVELS, 1)
    moved = pltpu.roll(both, ROWS, 1)
    coef_west[...] = twice_step * jnp.where(lane < ROWS, fm, jnp.where(lane < 2 * ROWS, moved, -moved))
    mu, fm, both, u = col_pack(1, LANES - 1)
    m, s = mu[LEVELS - 1], u[LEVELS - 1]
    for l in range(LEVELS - 1):
        m = jnp.where(level == l, mu[l], m)
        s = jnp.where(level == l, u[l], s)
    s = speed_coef * s * m
    dm = diffuse_coef * m
    own = both * jnp.where(lane < ROWS, s, dm)
    g = own + pltpu.roll(own, LANES - ROWS, 1)
    going_east = jnp.where(lane < ROWS, g, jnp.where(lane < 2 * ROWS, s, dm))
    pay_west[...] = halved(going_west)
    pay_east[...] = halved(going_east)
    face = jnp.where(lane < ROWS, -twice_step * s, twice_step * dm) * fm
    in_pres = (lane >= 2 * ROWS + 2 * LEVELS) & (lane < 2 * ROWS + 3 * LEVELS)
    coef_east[...] = jnp.where(
        lane < 2 * ROWS, face, jnp.where(in_pres, -twice_step * gravity * m, 0.0)
    )


def inner_kernel(
    total_rows,
    raw_bef, raw_cur, scalar_flags, east_flags, north_flags,
    after_v, filtered_v,
    cur_v, bef_v, pres_v, flux_v,
):
    height, width = raw_cur.shape[2], raw_cur.shape[3]
    n_chunks, n_tiles = height // SUBS, width // LANES
    lat = lax.axis_index("lat")
    flags = (scalar_flags, east_flags, north_flags)

    zero = jnp.zeros((SUBS, LANES), jnp.float32)
    lane = lane_ids((SUBS, LANES))
    sub = row_ids((SUBS, LANES))
    first_lane, last_lane = lane == 0, lane == LANES - 1
    tiles = [pl.ds(j * LANES, LANES) for j in range(n_tiles)]
    for l in range(LEVELS):
        for j in range(n_tiles):
            pres_v[l, j, pl.ds(height, SUBS), :] = zero
            for f in range(FIELDS):
                cur_v[f, l, j, pl.ds(height, SUBS), :] = zero
                bef_v[f, l, j, pl.ds(height, SUBS), :] = zero
                flux_v[f, l, j, pl.ds(0, SUBS), :] = zero

    def masked(c):
        rows = pl.ds(pl.multiple_of(c * SUBS, SUBS), SUBS)
        puts = []
        for j, cols in enumerate(tiles):
            total = zero
            for l in range(LEVELS):
                masks = [flags[t][l, rows, cols].astype(jnp.float32) for t in range(3)]
                cur = [raw_cur[f, l, rows, cols] * masks[mask_of(f)] for f in range(FIELDS)]
                rho = haline * cur[1] - thermal * cur[0]
                total = total + rho
                puts.append((pres_v, (l, j, rows), total - 0.5 * rho))
                for f in range(FIELDS):
                    puts.append((cur_v, (f, l, j, rows), cur[f]))
                    puts.append((bef_v, (f, l, j, rows), raw_bef[f, l, rows, cols] * masks[mask_of(f)]))
        return puts

    def store(puts):
        for ref, at, value in puts:
            ref[at] = value

    def east_of(x):
        beyond = x[1:] + [zero]
        return [pltpu.roll(jnp.where(first_lane, b, a), LANES - 1, 1) for a, b in zip(x, beyond)]

    def west_of(x):
        beyond = [zero] + x[:-1]
        return [pltpu.roll(jnp.where(last_lane, b, a), 1, 1) for a, b in zip(x, beyond)]

    def each(op, *xs):
        return [op(*x) for x in zip(*xs)]

    def face_flux(s, m, x, x_next, y, y_next):
        return each(lambda s, m, x, xn, y, yn: s * (x + xn) - m * (yn - y), s, m, x, x_next, y, y_next)

    def at(ref, r):
        return [ref[j, r, :] for j in range(n_tiles)]

    half = twice_step

    def north_fluxes(c):
        rows = pl.ds(pl.multiple_of(c * SUBS, SUBS), SUBS)
        shifted = pl.ds(c * SUBS + 1, SUBS)
        puts = []
        for l in range(LEVELS):
            s_n = [half * speed_coef * x for x in at(cur_v.at[3, l], rows)]
            m_n = [half * diffuse_coef * flags[2][l, rows, cols].astype(jnp.float32) for cols in tiles]
            for f in range(FIELDS):
                flux = face_flux(
                    s_n, m_n,
                    at(cur_v.at[f, l], rows), at(cur_v.at[f, l], shifted),
                    at(bef_v.at[f, l], rows), at(bef_v.at[f, l], shifted),
                )
                for j, x in enumerate(flux):
                    puts.append((flux_v, (f, l, j, pl.ds(pl.multiple_of((c + 1) * SUBS, SUBS), SUBS)), x))
        return puts

    def stepped(c):
        rows = pl.ds(pl.multiple_of(c * SUBS, SUBS), SUBS)
        shifted = pl.ds(c * SUBS + 1, SUBS)
        own_face = pl.ds(pl.multiple_of((c + 1) * SUBS, SUBS), SUBS)
        south_face = pl.ds((c + 1) * SUBS - 1, SUBS)
        index = (lat * height + c * SUBS + sub).astype(jnp.float32)
        cor = half * coriolis * (2.0 * (index + 0.5) / total_rows - 1.0)
        puts = []
        for l in range(LEVELS):
            masks = [[flags[t][l, rows, cols].astype(jnp.float32) for cols in tiles] for t in range(3)]
            cur = [at(cur_v.at[f, l], rows) for f in range(FIELDS)]
            bef = [at(bef_v.at[f, l], rows) for f in range(FIELDS)]
            pres = at(pres_v.at[l], rows)
            slope_e = each(lambda m, e, p: (half * gravity) * m * (e - p), masks[1], east_of(pres), pres)
            slope_n = each(lambda m, n, p: (half * gravity) * m * (n - p), masks[2], at(pres_v.at[l], shifted), pres)
            s_e, m_e = [half * speed_coef * x for x in cur[2]], [half * diffuse_coef * x for x in masks[1]]
            for f in range(FIELDS):
                flux_e = face_flux(s_e, m_e, cur[f], east_of(cur[f]), bef[f], east_of(bef[f]))
                flux_n = at(flux_v.at[f, l], own_face)
                flux_s = at(flux_v.at[f, l], south_face)
                tend = each(lambda w, e, s, n: (w - e) + (s - n), west_of(flux_e), flux_e, flux_s, flux_n)
                if f == 2:
                    tend = each(lambda t, v, g: t + (cor * v - g), tend, cur[3], slope_e)
                elif f == 3:
                    tend = each(lambda t, u, g: t - (cor * u + g), tend, cur[2], slope_n)
                new = each(lambda b, t, m: (b + t) * m, bef[f], tend, masks[mask_of(f)])
                mid = each(lambda c, b, n: (1.0 - 2.0 * asselin) * c + asselin * (b + n), cur[f], bef[f], new)
                for cols, a, x in zip(tiles, new, mid):
                    puts.append((after_v, (f, l, rows, cols), a))
                    puts.append((filtered_v, (f, l, rows, cols), x))
        return puts

    for c in range(2):
        store(masked(c))

    def chunk(c, carry):
        ahead = masked(jnp.minimum(c + 2, n_chunks - 1))
        faces = north_fluxes(c)
        store(ahead)
        store(faces)
        store(stepped(c))

        return carry

    lax.fori_loop(0, n_chunks, chunk, 0)


def rim_kernel(
    got_a, got_b, got_east, got_west, coef_north, coef_south, coef_west, coef_east,
    after_v, filtered_v,
    after, filtered, after_w, filtered_w,
    add_rows, add_cols, sems,
):
    height, width = after.shape[2], after.shape[3]
    n_chunks, n_tiles = height // SUBS, width // LANES
    lane = lane_ids((SUBS, LANES))
    sub = row_ids((SUBS, LANES))
    even = lax.axis_index("lat") % 2 == 0

    def out(i, rows, cols):
        copies = [
            pltpu.make_async_copy(s.at[:, :, rows, cols], d.at[:, :, rows, cols], sems.at[i, q])
            for q, (s, d) in enumerate(((after_w, after), (filtered_w, filtered)))
        ]
        for copy in copies:
            copy.start()
        return copies

    middle = pl.ds(SUBS, height - 2 * SUBS)
    pending = out(4, middle, pl.ds(LANES, width - 2 * LANES))

    for j in range(n_tiles):
        cols = pl.ds(j * LANES, LANES)
        got = [(got_a[pl.ds(q * SUBS, SUBS), cols], got_b[pl.ds((4 * j + q) * SUBS, SUBS), :]) for q in range(4)]
        north = [jnp.where(even, a, b) for a, b in got]
        south = [jnp.where(even, b, a) for a, b in got]

        def coef(ref, q):
            return ref[pl.ds(q * SUBS, SUBS), cols]

        rho = jnp.where(sub < LEVELS, haline * pltpu.roll(north[0], LEVELS, 0) - thermal * north[0], 0.0)
        total = rho + pltpu.roll(rho, 1, 0)
        total = total + pltpu.roll(total, 2, 0)
        pres = pltpu.roll(total - 0.5 * rho, LEVELS, 0)
        for h in range(2):
            at = pl.ds(h * SUBS, SUBS)
            up = coef(coef_north, h) * north[h] + coef(coef_north, 2 + h) * north[2 + h]
            if h == 1:
                up = up + coef(coef_north, 4) * pres
            add_rows[1, at, cols] = up
            add_rows[0, at, cols] = (
                coef(coef_south, h) * south[h]
                + coef(coef_south, 2 + h) * south[2]
                + coef(coef_south, 4 + h) * south[3]
            )

    def apply(f, l, rows, j, extra):
        cols = pl.ds(j * LANES, LANES)
        after_w[f, l, rows, cols] = after_v[f, l, rows, cols] + extra
        filtered_w[f, l, rows, cols] = filtered_v[f, l, rows, cols] + asselin * extra

    for side, (got, coef) in enumerate(((got_west[...], coef_west), (got_east[...], coef_east))):
        for part in range(2):
            rows = pl.ds(part * (height // 2), height // 2)
            x = got if part == 0 else pltpu.roll(got, LANES // 2, 1)
            x = x * coef[rows, :]
            add_cols[side, rows, :] = (
                x + pltpu.roll(x, LANES - ROWS, 1) + pltpu.roll(x, LANES - 2 * ROWS, 1)
            )

    def edge_cols(c):
        rows = pl.ds(pl.multiple_of(c * SUBS, SUBS), SUBS)
        return rows, add_cols[0, rows, :], add_cols[1, rows, :]

    def put(value, k, at):
        return jnp.where(lane == at, jnp.broadcast_to(value[:, k : k + 1], (SUBS, LANES)), 0.0)

    def row_chunk(c, side, line):
        rows, west, east = edge_cols(c)
        for f in range(FIELDS):
            for l in range(LEVELS):
                k = f * LEVELS + l
                for j in range(n_tiles):
                    row = add_rows[side, pl.ds(k, 1), pl.ds(j * LANES, LANES)]
                    extra = jnp.where(sub == line, jnp.broadcast_to(row, (SUBS, LANES)), 0.0)
                    if j == 0:
                        extra = extra + put(west, k, 0)
                    if j == n_tiles - 1:
                        extra = extra + put(east, k, LANES - 1)
                    apply(f, l, rows, j, extra)

    row_chunk(0, 0, 0)
    pending += out(0, pl.ds(0, SUBS), pl.ds(0, width))
    row_chunk(n_chunks - 1, 1, SUBS - 1)
    pending += out(1, pl.ds(height - SUBS, SUBS), pl.ds(0, width))

    def side_chunk(c, carry):
        rows, west, east = edge_cols(c)
        for f in range(FIELDS):
            for l in range(LEVELS):
                k = f * LEVELS + l
                apply(f, l, rows, 0, put(west, k, 0))
                apply(f, l, rows, n_tiles - 1, put(east, k, LANES - 1))
        return carry

    lax.fori_loop(1, n_chunks - 1, side_chunk, 0)
    pending += out(2, middle, pl.ds(0, LANES))
    pending += out(3, middle, pl.ds(width - LANES, LANES))
    for copy in pending:
        copy.wait()


def shards(n_lat, earlier_state, present_state, scalar_wet_flags, eastside_wet_flags, northside_wet_flags):
    args = (earlier_state, present_state, scalar_wet_flags, eastside_wet_flags, northside_wet_flags)
    height, width = present_state.shape[2:]
    n_lon = lax.axis_size("lon")
    f32 = jnp.float32
    params = pltpu.CompilerParams(vmem_limit_bytes=VMEM_LIMIT)
    state = (FIELDS, LEVELS, height, width)
    apart = (LEVELS, width // LANES, height + SUBS, LANES)

    def vmem(*shape):
        return pltpu.VMEM(shape, f32)

    edges = pl.pallas_call(
        functools.partial(edges_kernel, n_lat),
        out_shape=[
            vmem(2 * ROWS, width), vmem(2 * ROWS * (width // LANES), LANES),
            vmem(height // 2, LANES), vmem(height // 2, LANES),
            vmem(2 * ROWS + SUBS, width), vmem(3 * ROWS, width), vmem(height, LANES), vmem(height, LANES),
        ],
        in_specs=[ANY] * 5,
        out_specs=[VMEM] * 8,
        scratch_shapes=[
            pltpu.VMEM((2, 2, FIELDS, LEVELS, height, LANES), f32),
            pltpu.VMEM((2, 3, LEVELS, height, LANES), jnp.int32),
            pltpu.VMEM((2, 2, FIELDS, LEVELS, SUBS, width), f32),
            pltpu.VMEM((2, 3, LEVELS, SUBS, width), jnp.int32),
            pltpu.SemaphoreType.DMA((20,)),
        ],
        compiler_params=params,
        cost_estimate=pl.CostEstimate(flops=500_000, bytes_accessed=3_600_000, transcendentals=0),
        name="edges",
    )(*[pltpu.with_memory_space_constraint(x, pltpu.HBM) for x in args])
    pay_a, pay_b, pay_west, pay_east, *coefs = edges

    def device(lon, lat):
        return lon * n_lat + lat

    lons, lats, top = range(n_lon), range(n_lat), n_lat - 1
    pairs_a = [(device(lon, lat), device(lon, lat ^ 1)) for lon in lons for lat in lats]
    pairs_b = [
        (
            device(lon, lat),
            device(n_lon - 1 - lon, lat) if lat in (0, top) else device(lon, lat + 1 if lat % 2 else lat - 1),
        )
        for lon in lons
        for lat in lats
    ]
    got_b = lax.ppermute(pay_b, ("lon", "lat"), pairs_b)
    got_a = lax.ppermute(pay_a, ("lon", "lat"), pairs_a)
    got_east = lax.ppermute(pay_west, "lon", [(i, (i - 1) % n_lon) for i in lons])
    got_west = lax.ppermute(pay_east, "lon", [(i, (i + 1) % n_lon) for i in lons])

    after_v, filtered_v = pl.pallas_call(
        functools.partial(inner_kernel, height * n_lat),
        out_shape=[vmem(*state), vmem(*state)],
        in_specs=[VMEM] * 5,
        out_specs=[VMEM, VMEM],
        scratch_shapes=[
            pltpu.VMEM((FIELDS, *apart), f32),
            pltpu.VMEM((FIELDS, *apart), f32),
            pltpu.VMEM(apart, f32),
            pltpu.VMEM((FIELDS, *apart), f32),
        ],
        compiler_params=params,
        cost_estimate=pl.CostEstimate(flops=20_000_000, bytes_accessed=9_000_000, transcendentals=0),
        name="inner",
    )(*[pltpu.with_memory_space_constraint(x, pltpu.VMEM) for x in args])

    def in_vmem(x):
        return pltpu.with_memory_space_constraint(x, pltpu.VMEM)

    fixed = [in_vmem(x) for x in (got_a, got_b, got_east, got_west, *coefs, after_v, filtered_v)]
    after, filtered, _, _ = pl.pallas_call(
        rim_kernel,
        out_shape=[pltpu.HBM(state, f32), pltpu.HBM(state, f32), vmem(*state), vmem(*state)],
        in_specs=[VMEM] * 10,
        out_specs=[ANY, ANY, VMEM, VMEM],
        scratch_shapes=[
            pltpu.VMEM((2, ROWS, width), f32),
            pltpu.VMEM((2, height, LANES), f32),
            pltpu.SemaphoreType.DMA((5, 2)),
        ],
        input_output_aliases={8: 2, 9: 3},
        compiler_params=params,
        cost_estimate=pl.CostEstimate(flops=500_000, bytes_accessed=3_000_000, transcendentals=0),
        name="rim",
    )(*fixed)
    return after, filtered


def solution(mesh):
    placed = (
        P(None, None, "lat", "lon"),
        P(None, None, "lat", "lon"),
        P(None, "lat", "lon"),
        P(None, "lat", "lon"),
        P(None, "lat", "lon"),
    )
    return jax.shard_map(
        functools.partial(shards, mesh.shape["lat"]),
        mesh=mesh,
        in_specs=placed,
        out_specs=(P(None, None, "lat", "lon"), P(None, None, "lat", "lon")),
        check_vma=False,
    )
```

```python
import functools

import jax
import jax.numpy as jnp
from jax import lax
from jax.experimental import pallas as pl
from jax.experimental.pallas import tpu as pltpu
from jax.sharding import PartitionSpec as P

advect_coef = 0.5
diffuse_coef = 0.25
twice_step = 0.5
gravity = 0.5
coriolis = 0.5
thermal = 0.2
haline = 0.15
asselin = 0.1

LANES = 128
SUBS = 8
FIELDS = 4
LEVELS = 4
ROWS = FIELDS * LEVELS
VMEM_LIMIT = 24 * 1024 * 1024

speed_coef = advect_coef * 0.5
ANY = pl.BlockSpec(memory_space=pl.ANY)
VMEM = pl.BlockSpec(memory_space=pltpu.VMEM)


def mask_of(field):
    return max(field - 1, 0)


def lane_ids(shape):
    return lax.broadcasted_iota(jnp.int32, shape, len(shape) - 1)


def row_ids(shape):
    return lax.broadcasted_iota(jnp.int32, shape, len(shape) - 2)


def edges_kernel(
    n_lat,
    earlier, present, scalar_flags, east_flags, north_flags,
    pay_a, pay_b, pay_west, pay_east, coef_north, coef_south, coef_west, coef_east,
    col_state, col_flag, row_state, row_flag, sems,
):
    height, width = present.shape[2], present.shape[3]
    lat = lax.axis_index("lat")
    flags = (scalar_flags, east_flags, north_flags)
    copies = []
    for side in range(2):
        cols = pl.ds(0 if side == 0 else width - LANES, LANES)
        for t, state in enumerate((present, earlier)):
            copies.append((state.at[:, :, :, cols], col_state.at[side, t]))
        for t, flag in enumerate(flags):
            copies.append((flag.at[:, :, cols], col_flag.at[side, t]))
    for side in range(2):
        rows = pl.ds(0 if side == 0 else height - SUBS, SUBS)
        for t, state in enumerate((present, earlier)):
            copies.append((state.at[:, :, rows, :], row_state.at[side, t]))
        for t, flag in enumerate(flags):
            copies.append((flag.at[:, rows, :], row_flag.at[side, t]))
    copies = [
        pltpu.make_async_copy(src, dst, sems.at[i]) for i, (src, dst) in enumerate(copies)
    ]
    for copy in copies:
        copy.start()
    n_tiles = width // LANES
    lane = lane_ids((SUBS, LANES))
    sub = row_ids((SUBS, LANES))

    for copy in copies[:10]:
        copy.wait()

    base, level = lane & (ROWS - 1), lane & (LEVELS - 1)
    zeros = jnp.zeros((SUBS, LANES), jnp.float32)
    tiles = range(height // SUBS)

    def columns(x, at):
        return [jnp.broadcast_to(x[r * SUBS : (r + 1) * SUBS, at : at + 1], (SUBS, LANES)) for r in tiles]

    def placed(where, xs, old):
        return [jnp.where(where, x, o) for x, o in zip(xs, old)]

    def col_pack(side, at):
        fm, both, extra, u, total = ([zeros] * len(tiles) for _ in range(5))
        for l in range(LEVELS):
            mask = [columns(col_flag[side, t, l].astype(jnp.float32), at) for t in range(3)]
            for f in range(FIELDS):
                fm = placed(base == f * LEVELS + l, mask[mask_of(f)], fm)
            now = []
            for f in range(FIELDS):
                now.append(columns(col_state[side, 0, f, l], at))
                both = placed(lane == f * LEVELS + l, now[f], both)
                both = placed(lane == ROWS + f * LEVELS + l, columns(col_state[side, 1, f, l], at), both)
            if side == 0:
                rho = [(haline * s - thermal * t) * m for s, t, m in zip(now[1], now[0], mask[0])]
                total = [a + b for a, b in zip(total, rho)]
                pres = [a - 0.5 * b for a, b in zip(total, rho)]
                extra = placed(lane == 2 * ROWS + 2 * LEVELS + l, pres, extra)
            else:
                extra = placed(level == l, mask[1], extra)
                u = placed(level == l, now[2], u)
        return zip(fm, both, extra, u)

    in_pres = (lane >= 2 * ROWS + 2 * LEVELS) & (lane < 2 * ROWS + 3 * LEVELS)
    going_west, going_east, coefs_west, coefs_east = [], [], [], []
    for fm, both, pres, _ in col_pack(0, 0):
        both = both * fm
        moved = pltpu.roll(both, ROWS, 1)
        going_west.append(both + pres)
        coefs_west.append(twice_step * jnp.where(lane < ROWS, fm, jnp.where(lane < 2 * ROWS, moved, -moved)))
    for fm, both, mu, u in col_pack(1, LANES - 1):
        s, dm = speed_coef * u * mu, diffuse_coef * mu
        own = both * fm * jnp.where(lane < ROWS, s, dm)
        g = own + pltpu.roll(own, LANES - ROWS, 1)
        going_east.append(jnp.where(lane < ROWS, g, jnp.where(lane < 2 * ROWS, s, dm)))
        face = jnp.where(lane < ROWS, -twice_step * s, twice_step * dm) * fm
        coefs_east.append(
            jnp.where(lane < 2 * ROWS, face, jnp.where(in_pres, -twice_step * gravity * mu, 0.0))
        )
    half = len(tiles) // 2
    folded = [
        [jnp.where(lane < LANES // 2, x[r], pltpu.roll(x[r + half], LANES // 2, 1)) for r in range(half)]
        for x in (going_west, going_east)
    ]
    for r in tiles:
        rows = pl.ds(r * SUBS, SUBS)
        coef_west[rows, :] = coefs_west[r]
        coef_east[rows, :] = coefs_east[r]
        if r < half:
            pay_west[rows, :] = folded[0][r]
            pay_east[rows, :] = folded[1][r]

    for copy in copies[10:]:
        copy.wait()

    def row_pack(side, at, j):
        line = pl.ds(at, 1)
        cols = pl.ds(j * LANES, LANES)

        def gather(rows):
            packed = jnp.broadcast_to(rows[0], (SUBS, LANES))
            for k in range(1, SUBS):
                packed = jnp.where(sub == k, jnp.broadcast_to(rows[k], (SUBS, LANES)), packed)
            return packed

        def flag_row(t, l):
            return row_flag[side, t, l, line, cols].astype(jnp.float32)

        fm = [
            gather([flag_row(mask_of(f), l) for f in (2 * h, 2 * h + 1) for l in range(LEVELS)])
            for h in range(2)
        ]
        cur, bef = (
            [
                fm[h]
                * gather([row_state[side, t, f, l, line, cols] for f in (2 * h, 2 * h + 1) for l in range(LEVELS)])
                for h in range(2)
            ]
            for t in range(2)
        )
        return fm, cur, bef

    back = LANES - 1 - lane
    pay_b[pl.ds(2 * ROWS * n_tiles, SUBS), :] = jnp.zeros((SUBS, LANES), jnp.float32)
    even = lat % 2 == 0
    is_top = lat == n_lat - 1
    for j in range(n_tiles):
        cols = pl.ds(j * LANES, LANES)
        fm, cur, bef = row_pack(1, SUBS - 1, j)
        low_v = pltpu.roll(cur[1], 4, 0)
        s = speed_coef * jnp.where(sub < 4, low_v, cur[1])
        m = diffuse_coef * jnp.where(sub < 4, pltpu.roll(fm[1], 4, 0), fm[1])
        g = [s * cur[h] + m * bef[h] for h in range(2)]
        for h in range(2):
            at = pl.ds(h * SUBS, SUBS)
            coef_north[at, cols] = -twice_step * fm[h] * s
            coef_north[pl.ds(ROWS + h * SUBS, SUBS), cols] = twice_step * fm[h] * m
        coef_north[pl.ds(2 * ROWS, SUBS), cols] = jnp.where(sub < 4, 0.0, -twice_step * gravity * fm[1])

        fm_s, cur_s, bef_s = row_pack(0, 0, j)
        for h in range(2):
            at = pl.ds(h * SUBS, SUBS)
            coef_south[at, cols] = twice_step * fm_s[h]
            coef_south[pl.ds(ROWS + h * SUBS, SUBS), cols] = twice_step * cur_s[h]
            coef_south[pl.ds(2 * ROWS + h * SUBS, SUBS), cols] = -twice_step * bef_s[h]

        north_going = g + [s, m]
        south_going = cur_s + bef_s
        for q in range(4):
            at = pl.ds(q * SUBS, SUBS)
            pay_a[at, cols] = jnp.where(even, north_going[q], south_going[q])

        @pl.when(jnp.logical_not(is_top))
        def _():
            for q in range(4):
                below = jnp.where(lat == 0, 0.0, south_going[q])
                pay_b[pl.ds((4 * j + q) * SUBS, SUBS), :] = jnp.where(even, below, north_going[q])

        @pl.when(is_top)
        def _():
            for q, x in enumerate(cur + bef):
                mirrored = pl.ds((4 * (n_tiles - 1 - j) + q) * SUBS, SUBS)
                turned = jnp.take_along_axis(x, back, axis=1)
                pay_b[mirrored, :] = turned if q % 2 == 0 else -turned


def inner_kernel(
    total_rows,
    raw_bef, raw_cur, scalar_flags, east_flags, north_flags,
    after_v, filtered_v,
    cur_v, bef_v, pres_v, flux_v,
):
    height, width = raw_cur.shape[2], raw_cur.shape[3]
    n_chunks, n_tiles = height // SUBS, width // LANES
    lat = lax.axis_index("lat")
    flags = (scalar_flags, east_flags, north_flags)

    zero = jnp.zeros((SUBS, LANES), jnp.float32)
    lane = lane_ids((SUBS, LANES))
    sub = row_ids((SUBS, LANES))
    first_lane, last_lane = lane == 0, lane == LANES - 1
    last_sub = sub == SUBS - 1
    tiles = [pl.ds(j * LANES, LANES) for j in range(n_tiles)]
    for l in range(LEVELS):
        for j in range(n_tiles):
            pres_v[l, j, pl.ds(height, SUBS), :] = zero
            for f in range(FIELDS):
                cur_v[f, l, j, pl.ds(height, SUBS), :] = zero
                bef_v[f, l, j, pl.ds(height, SUBS), :] = zero
                flux_v[f, l, j] = zero

    def store(puts):
        for ref, at, value in puts:
            ref[at] = value

    def each(op, *xs):
        return [op(*x) for x in zip(*xs)]

    def east_of(x):
        return [
            pltpu.roll(jnp.where(first_lane, b, a), LANES - 1, 1) for a, b in zip(x, x[1:] + [zero])
        ]

    def west_of(x):
        return [pltpu.roll(jnp.where(last_lane, b, a), 1, 1) for a, b in zip(x, [zero] + x[:-1])]

    def south_of(x, below):
        return [pltpu.roll(jnp.where(last_sub, b, a), 1, 0) for a, b in zip(x, below)]

    def face_flux(s, m, x, x_next, y, y_next):
        return each(lambda s, m, x, xn, y, yn: s * (x + xn) - m * (yn - y), s, m, x, x_next, y, y_next)

    def at(ref, r):
        return [ref[j, r, :] for j in range(n_tiles)]

    half = twice_step

    def unit(c, l, fields):
        rows = pl.ds(pl.multiple_of(c * SUBS, SUBS), SUBS)
        shifted = pl.ds(c * SUBS + 1, SUBS)

        def flag(t):
            return [flags[t][l, rows, cols].astype(jnp.float32) for cols in tiles]

        cur_e = {f: east_of(at(cur_v.at[f, l], rows)) for f in fields}
        bef_e = {f: east_of(at(bef_v.at[f, l], rows)) for f in fields}
        pres_e = east_of(at(pres_v.at[l], rows)) if 2 in fields else None
        yield []
        s_e, m_e = [half * speed_coef * x for x in at(cur_v.at[2, l], rows)], [half * diffuse_coef * x for x in flag(1)]
        s_n, m_n = [half * speed_coef * x for x in at(cur_v.at[3, l], rows)], [half * diffuse_coef * x for x in flag(2)]
        puts, own, west, south = [], {}, {}, {}
        for f in fields:
            cur, bef = at(cur_v.at[f, l], rows), at(bef_v.at[f, l], rows)
            flux_e = face_flux(s_e, m_e, cur, cur_e[f], bef, bef_e[f])
            flux_n = face_flux(s_n, m_n, cur, at(cur_v.at[f, l], shifted), bef, at(bef_v.at[f, l], shifted))
            west[f] = west_of(flux_e)
            south[f] = south_of(flux_n, at(flux_v.at[f, l], slice(None)))
            own[f] = each(lambda e, n: e + n, flux_e, flux_n)
            puts += [(flux_v, (f, l, j), x) for j, x in enumerate(flux_n)]
        yield puts
        puts = []
        for f in fields:
            cur, bef = at(cur_v.at[f, l], rows), at(bef_v.at[f, l], rows)
            mask = flag(mask_of(f))
            tend = each(lambda w, s, o: (w + s) - o, west[f], south[f], own[f])
            if f >= 2:
                index = (lat * height + c * SUBS + sub).astype(jnp.float32)
                cor = half * coriolis * (2.0 * (index + 0.5) / total_rows - 1.0)
                pres = at(pres_v.at[l], rows)
                ahead = pres_e if f == 2 else at(pres_v.at[l], shifted)
                slope = each(lambda m, a, p: (half * gravity) * m * (a - p), mask, ahead, pres)
                if f == 2:
                    tend = each(lambda t, v, g: t + (cor * v - g), tend, at(cur_v.at[3, l], rows), slope)
                else:
                    tend = each(lambda t, u, g: t - (cor * u + g), tend, at(cur_v.at[2, l], rows), slope)
            new = each(lambda b, t, m: (b + t) * m, bef, tend, mask)
            mid = each(lambda c, b, n: (1.0 - 2.0 * asselin) * c + asselin * (b + n), cur, bef, new)
            for cols, a, x in zip(tiles, new, mid):
                puts.append((after_v, (f, l, rows, cols), a))
                puts.append((filtered_v, (f, l, rows, cols), x))
        yield puts

    def masking(c):
        rows = pl.ds(pl.multiple_of(c * SUBS, SUBS), SUBS)
        totals = [zero] * n_tiles
        for l in range(LEVELS):
            for part in (range(0, n_tiles // 2), range(n_tiles // 2, n_tiles)):
                puts = []
                for j in part:
                    cols = tiles[j]
                    masks = [flags[t][l, rows, cols].astype(jnp.float32) for t in range(3)]
                    cur = [raw_cur[f, l, rows, cols] * masks[mask_of(f)] for f in range(FIELDS)]
                    rho = haline * cur[1] - thermal * cur[0]
                    totals[j] = totals[j] + rho
                    puts.append((pres_v, (l, j, rows), totals[j] - 0.5 * rho))
                    for f in range(FIELDS):
                        puts.append((cur_v, (f, l, j, rows), cur[f]))
                        puts.append((bef_v, (f, l, j, rows), raw_bef[f, l, rows, cols] * masks[mask_of(f)]))
                yield puts

    for c in range(2):
        for puts in masking(c):
            store(puts)

    def two_chunks(i, carry):
        units = [unit(2 * i + k, l, fields) for k in range(2) for l in range(LEVELS) for fields in ((0, 1), (2, 3))]
        later = [masking(jnp.minimum(2 * i + 2 + k, n_chunks - 1)) for k in range(2)]
        per_chunk = len(units) // 2
        for t in range(len(units) + 2):
            puts = []
            for u in (t, t - 1, t - 2):
                if 0 <= u < len(units):
                    puts += next(units[u])
            if t < len(units):
                puts += next(later[t // per_chunk])
            store(puts)
        return carry

    lax.fori_loop(0, n_chunks // 2, two_chunks, 0)


def rim_kernel(
    got_a, got_b, got_east, got_west, coef_north, coef_south, coef_west, coef_east,
    after_v, filtered_v,
    after, filtered, after_w, filtered_w,
    add_rows, add_cols, sems,
):
    height, width = after.shape[2], after.shape[3]
    n_chunks, n_tiles = height // SUBS, width // LANES
    lane = lane_ids((SUBS, LANES))
    sub = row_ids((SUBS, LANES))
    even = lax.axis_index("lat") % 2 == 0

    def out(i, rows, cols):
        copies = [
            pltpu.make_async_copy(s.at[:, :, rows, cols], d.at[:, :, rows, cols], sems.at[i, q])
            for q, (s, d) in enumerate(((after_w, after), (filtered_w, filtered)))
        ]
        for copy in copies:
            copy.start()
        return copies

    middle = pl.ds(SUBS, height - 2 * SUBS)
    pending = out(2, middle, pl.ds(LANES, width - 2 * LANES))

    for j in range(n_tiles):
        cols = pl.ds(j * LANES, LANES)
        got = [(got_a[pl.ds(q * SUBS, SUBS), cols], got_b[pl.ds((4 * j + q) * SUBS, SUBS), :]) for q in range(4)]
        north = [jnp.where(even, a, b) for a, b in got]
        south = [jnp.where(even, b, a) for a, b in got]

        def coef(ref, q):
            return ref[pl.ds(q * SUBS, SUBS), cols]

        rho = jnp.where(sub < LEVELS, haline * pltpu.roll(north[0], LEVELS, 0) - thermal * north[0], 0.0)
        total = rho + pltpu.roll(rho, 1, 0)
        total = total + pltpu.roll(total, 2, 0)
        pres = pltpu.roll(total - 0.5 * rho, LEVELS, 0)
        for h in range(2):
            at = pl.ds(h * SUBS, SUBS)
            up = coef(coef_north, h) * north[h] + coef(coef_north, 2 + h) * north[2 + h]
            if h == 1:
                up = up + coef(coef_north, 4) * pres
            add_rows[1, at, cols] = up
            add_rows[0, at, cols] = (
                coef(coef_south, h) * south[h]
                + coef(coef_south, 2 + h) * south[2]
                + coef(coef_south, 4 + h) * south[3]
            )

    for side, (got, coef) in enumerate(((got_west[...], coef_west), (got_east[...], coef_east))):
        for part in range(2):
            rows = pl.ds(part * (height // 2), height // 2)
            x = got if part == 0 else pltpu.roll(got, LANES // 2, 1)
            x = x * coef[rows, :]
            add_cols[side, rows, :] = (
                x + pltpu.roll(x, LANES - ROWS, 1) + pltpu.roll(x, LANES - 2 * ROWS, 1)
            )

    def edge_cols(rows):
        return add_cols[0, rows, :], add_cols[1, rows, :]

    def put(value, k, at):
        return jnp.where(lane == at, jnp.broadcast_to(value[:, k : k + 1], (SUBS, LANES)), 0.0)

    def apply(extras):
        sums = [(at, after_v[at] + x, filtered_v[at] + asselin * x) for at, x in extras]
        for at, new, mid in sums:
            after_w[at] = new
            filtered_w[at] = mid

    def row_chunk(c, side, line):
        rows = pl.ds(c * SUBS, SUBS)
        west, east = edge_cols(rows)
        for f in range(FIELDS):
            extras = []
            for l in range(LEVELS):
                k = f * LEVELS + l
                for j in range(n_tiles):
                    cols = pl.ds(j * LANES, LANES)
                    extra = jnp.where(sub == line, jnp.broadcast_to(add_rows[side, pl.ds(k, 1), cols], (SUBS, LANES)), 0.0)
                    if j == 0:
                        extra = extra + put(west, k, 0)
                    if j == n_tiles - 1:
                        extra = extra + put(east, k, LANES - 1)
                    extras.append(((f, l, rows, cols), extra))
            apply(extras)

    def side_chunk(c):
        first, last = pl.ds(0, LANES), pl.ds(width - LANES, LANES)
        tiles = [pl.ds(pl.multiple_of(r * SUBS, SUBS), SUBS) for r in (c, c + 1)]
        edges = [edge_cols(rows) for rows in tiles]
        for f in range(FIELDS):
            extras = []
            for l in range(LEVELS):
                k = f * LEVELS + l
                for rows, (west, east) in zip(tiles, edges):
                    extras.append(((f, l, rows, first), put(west, k, 0)))
                    extras.append(((f, l, rows, last), put(east, k, LANES - 1)))
            apply(extras)

    row_chunk(0, 0, 0)
    pending += out(0, pl.ds(0, SUBS), pl.ds(0, width))
    row_chunk(n_chunks - 1, 1, SUBS - 1)
    pending += out(1, pl.ds(height - SUBS, SUBS), pl.ds(0, width))
    for c in range(1, n_chunks - 1, 2):
        side_chunk(c)
        rows = pl.ds(c * SUBS, 2 * SUBS)
        pending += out(2 + c, rows, pl.ds(0, LANES))
        pending += out(3 + c, rows, pl.ds(width - LANES, LANES))
    for copy in pending:
        copy.wait()


def shards(n_lat, earlier_state, present_state, scalar_wet_flags, eastside_wet_flags, northside_wet_flags):
    args = (earlier_state, present_state, scalar_wet_flags, eastside_wet_flags, northside_wet_flags)
    height, width = present_state.shape[2:]
    n_lon = lax.axis_size("lon")
    f32 = jnp.float32
    params = pltpu.CompilerParams(vmem_limit_bytes=VMEM_LIMIT)
    state = (FIELDS, LEVELS, height, width)
    apart = (LEVELS, width // LANES, height + SUBS, LANES)

    def vmem(*shape):
        return pltpu.VMEM(shape, f32)

    edges = pl.pallas_call(
        functools.partial(edges_kernel, n_lat),
        out_shape=[
            vmem(2 * ROWS, width), vmem(2 * ROWS * (width // LANES) + SUBS, LANES),
            vmem(height // 2, LANES), vmem(height // 2, LANES),
            vmem(2 * ROWS + SUBS, width), vmem(3 * ROWS, width), vmem(height, LANES), vmem(height, LANES),
        ],
        in_specs=[ANY] * 5,
        out_specs=[VMEM] * 8,
        scratch_shapes=[
            pltpu.VMEM((2, 2, FIELDS, LEVELS, height, LANES), f32),
            pltpu.VMEM((2, 3, LEVELS, height, LANES), jnp.int32),
            pltpu.VMEM((2, 2, FIELDS, LEVELS, SUBS, width), f32),
            pltpu.VMEM((2, 3, LEVELS, SUBS, width), jnp.int32),
            pltpu.SemaphoreType.DMA((20,)),
        ],
        compiler_params=params,
        cost_estimate=pl.CostEstimate(flops=500_000, bytes_accessed=3_600_000, transcendentals=0),
        name="edges",
    )(*[pltpu.with_memory_space_constraint(x, pltpu.HBM) for x in args])
    pay_a, pay_b, pay_west, pay_east, *coefs = edges

    def device(lon, lat):
        return lon * n_lat + lat

    lons, lats, top = range(n_lon), range(n_lat), n_lat - 1
    pairs_a = [(device(lon, lat), device(lon, lat ^ 1)) for lon in lons for lat in lats]
    pairs_b = [
        (
            device(lon, lat),
            device(n_lon - 1 - lon, lat) if lat in (0, top) else device(lon, lat + 1 if lat % 2 else lat - 1),
        )
        for lon in lons
        for lat in lats
    ]
    got_b = lax.ppermute(pay_b, ("lon", "lat"), pairs_b)
    got_a = lax.ppermute(pay_a, ("lon", "lat"), pairs_a)
    got_east = lax.ppermute(pay_west, "lon", [(i, (i - 1) % n_lon) for i in lons])
    got_west = lax.ppermute(pay_east, "lon", [(i, (i + 1) % n_lon) for i in lons])

    after_v, filtered_v = pl.pallas_call(
        functools.partial(inner_kernel, height * n_lat),
        out_shape=[vmem(*state), vmem(*state)],
        in_specs=[VMEM] * 5,
        out_specs=[VMEM, VMEM],
        scratch_shapes=[
            pltpu.VMEM((FIELDS, *apart), f32),
            pltpu.VMEM((FIELDS, *apart), f32),
            pltpu.VMEM(apart, f32),
            pltpu.VMEM((FIELDS, LEVELS, width // LANES, SUBS, LANES), f32),
        ],
        compiler_params=params,
        cost_estimate=pl.CostEstimate(flops=20_000_000, bytes_accessed=9_000_000, transcendentals=0),
        name="inner",
    )(*[pltpu.with_memory_space_constraint(x, pltpu.VMEM) for x in args])

    def in_vmem(x):
        return pltpu.with_memory_space_constraint(x, pltpu.VMEM)

    fixed = [in_vmem(x) for x in (got_a, got_b, got_east, got_west, *coefs, after_v, filtered_v)]
    after, filtered, _, _ = pl.pallas_call(
        rim_kernel,
        out_shape=[pltpu.HBM(state, f32), pltpu.HBM(state, f32), vmem(*state), vmem(*state)],
        in_specs=[VMEM] * 10,
        out_specs=[ANY, ANY, VMEM, VMEM],
        scratch_shapes=[
            pltpu.VMEM((2, ROWS, width), f32),
            pltpu.VMEM((2, height, LANES), f32),
            pltpu.SemaphoreType.DMA((3 + height // SUBS, 2)),
        ],
        input_output_aliases={8: 2, 9: 3},
        compiler_params=params,
        cost_estimate=pl.CostEstimate(flops=500_000, bytes_accessed=3_000_000, transcendentals=0),
        name="rim",
    )(*fixed)
    return after, filtered


def solution(mesh):
    placed = (
        P(None, None, "lat", "lon"),
        P(None, None, "lat", "lon"),
        P(None, "lat", "lon"),
        P(None, "lat", "lon"),
        P(None, "lat", "lon"),
    )
    return jax.shard_map(
        functools.partial(shards, mesh.shape["lat"]),
        mesh=mesh,
        in_specs=placed,
        out_specs=(P(None, None, "lat", "lon"), P(None, None, "lat", "lon")),
        check_vma=False,
    )
```

```python
import functools

import jax
import jax.numpy as jnp
from jax import lax
from jax.experimental import pallas as pl
from jax.experimental.pallas import tpu as pltpu
from jax.sharding import PartitionSpec as P

advect_coef = 0.5
diffuse_coef = 0.25
twice_step = 0.5
gravity = 0.5
coriolis = 0.5
thermal = 0.2
haline = 0.15
asselin = 0.1

LANES = 128
SUBS = 8
FIELDS = 4
LEVELS = 4
ROWS = FIELDS * LEVELS
VMEM_LIMIT = 24 * 1024 * 1024

speed_coef = advect_coef * 0.5
ANY = pl.BlockSpec(memory_space=pl.ANY)
VMEM = pl.BlockSpec(memory_space=pltpu.VMEM)


def mask_of(field):
    return max(field - 1, 0)


def lane_ids(shape):
    return lax.broadcasted_iota(jnp.int32, shape, len(shape) - 1)


def row_ids(shape):
    return lax.broadcasted_iota(jnp.int32, shape, len(shape) - 2)


def edges_kernel(
    n_lat,
    earlier, present, scalar_flags, east_flags, north_flags,
    pay_a, pay_b, pay_west, pay_east, coef_north, coef_south, coef_west, coef_east,
    col_state, col_flag, row_state, row_flag, sems,
):
    height, width = present.shape[2], present.shape[3]
    lat = lax.axis_index("lat")
    flags = (scalar_flags, east_flags, north_flags)
    copies = []
    for side in range(2):
        cols = pl.ds(0 if side == 0 else width - LANES, LANES)
        for t, state in enumerate((present, earlier)):
            copies.append((state.at[:, :, :, cols], col_state.at[side, t]))
        for t, flag in enumerate(flags):
            copies.append((flag.at[:, :, cols], col_flag.at[side, t]))
    for side in range(2):
        rows = pl.ds(0 if side == 0 else height - SUBS, SUBS)
        for t, state in enumerate((present, earlier)):
            copies.append((state.at[:, :, rows, :], row_state.at[side, t]))
        for t, flag in enumerate(flags):
            copies.append((flag.at[:, rows, :], row_flag.at[side, t]))
    copies = [
        pltpu.make_async_copy(src, dst, sems.at[i]) for i, (src, dst) in enumerate(copies)
    ]
    for copy in copies:
        copy.start()
    n_tiles = width // LANES
    lane = lane_ids((SUBS, LANES))
    sub = row_ids((SUBS, LANES))

    for copy in copies[:10]:
        copy.wait()

    base, level = lane & (ROWS - 1), lane & (LEVELS - 1)
    zeros = jnp.zeros((SUBS, LANES), jnp.float32)
    tiles = range(height // SUBS)

    def columns(x, at):
        return [jnp.broadcast_to(x[r * SUBS : (r + 1) * SUBS, at : at + 1], (SUBS, LANES)) for r in tiles]

    def placed(where, xs, old):
        return [jnp.where(where, x, o) for x, o in zip(xs, old)]

    def col_pack(side, at):
        fm, both, extra, u, total = ([zeros] * len(tiles) for _ in range(5))
        for l in range(LEVELS):
            mask = [columns(col_flag[side, t, l].astype(jnp.float32), at) for t in range(3)]
            for f in range(FIELDS):
                fm = placed(base == f * LEVELS + l, mask[mask_of(f)], fm)
            now = []
            for f in range(FIELDS):
                now.append(columns(col_state[side, 0, f, l], at))
                both = placed(lane == f * LEVELS + l, now[f], both)
                both = placed(lane == ROWS + f * LEVELS + l, columns(col_state[side, 1, f, l], at), both)
            if side == 0:
                rho = [(haline * s - thermal * t) * m for s, t, m in zip(now[1], now[0], mask[0])]
                total = [a + b for a, b in zip(total, rho)]
                pres = [a - 0.5 * b for a, b in zip(total, rho)]
                extra = placed(lane == 2 * ROWS + 2 * LEVELS + l, pres, extra)
            else:
                extra = placed(level == l, mask[1], extra)
                u = placed(level == l, now[2], u)
        return zip(fm, both, extra, u)

    in_pres = (lane >= 2 * ROWS + 2 * LEVELS) & (lane < 2 * ROWS + 3 * LEVELS)
    going_west, going_east, coefs_west, coefs_east = [], [], [], []
    for fm, both, pres, _ in col_pack(0, 0):
        both = both * fm
        moved = pltpu.roll(both, ROWS, 1)
        going_west.append(both + pres)
        coefs_west.append(twice_step * jnp.where(lane < ROWS, fm, jnp.where(lane < 2 * ROWS, moved, -moved)))
    for fm, both, mu, u in col_pack(1, LANES - 1):
        s, dm = speed_coef * u * mu, diffuse_coef * mu
        own = both * fm * jnp.where(lane < ROWS, s, dm)
        g = own + pltpu.roll(own, LANES - ROWS, 1)
        going_east.append(jnp.where(lane < ROWS, g, jnp.where(lane < 2 * ROWS, s, dm)))
        face = jnp.where(lane < ROWS, -twice_step * s, twice_step * dm) * fm
        coefs_east.append(
            jnp.where(lane < 2 * ROWS, face, jnp.where(in_pres, -twice_step * gravity * mu, 0.0))
        )
    half = len(tiles) // 2
    folded = [
        [jnp.where(lane < LANES // 2, x[r], pltpu.roll(x[r + half], LANES // 2, 1)) for r in range(half)]
        for x in (going_west, going_east)
    ]
    for r in tiles:
        rows = pl.ds(r * SUBS, SUBS)
        coef_west[rows, :] = coefs_west[r]
        coef_east[rows, :] = coefs_east[r]
        if r < half:
            pay_west[rows, :] = folded[0][r]
            pay_east[rows, :] = folded[1][r]

    for copy in copies[10:]:
        copy.wait()

    def row_pack(side, at, j):
        line = pl.ds(at, 1)
        cols = pl.ds(j * LANES, LANES)

        def gather(rows):
            packed = jnp.broadcast_to(rows[0], (SUBS, LANES))
            for k in range(1, SUBS):
                packed = jnp.where(sub == k, jnp.broadcast_to(rows[k], (SUBS, LANES)), packed)
            return packed

        def flag_row(t, l):
            return row_flag[side, t, l, line, cols].astype(jnp.float32)

        fm = [
            gather([flag_row(mask_of(f), l) for f in (2 * h, 2 * h + 1) for l in range(LEVELS)])
            for h in range(2)
        ]
        cur, bef = (
            [
                fm[h]
                * gather([row_state[side, t, f, l, line, cols] for f in (2 * h, 2 * h + 1) for l in range(LEVELS)])
                for h in range(2)
            ]
            for t in range(2)
        )
        return fm, cur, bef

    back = LANES - 1 - lane
    even = lat % 2 == 0
    is_top = lat == n_lat - 1
    puts = [(pay_b, pl.ds(2 * ROWS * n_tiles, SUBS), slice(None), zeros)]
    into_b, folded = [], []
    for j in range(n_tiles):
        cols = pl.ds(j * LANES, LANES)
        fm, cur, bef = row_pack(1, SUBS - 1, j)
        s = speed_coef * jnp.where(sub < 4, pltpu.roll(cur[1], 4, 0), cur[1])
        m = diffuse_coef * jnp.where(sub < 4, pltpu.roll(fm[1], 4, 0), fm[1])
        g = [s * cur[h] + m * bef[h] for h in range(2)]
        for h in range(2):
            puts.append((coef_north, pl.ds(h * SUBS, SUBS), cols, -twice_step * fm[h] * s))
            puts.append((coef_north, pl.ds(ROWS + h * SUBS, SUBS), cols, twice_step * fm[h] * m))
        puts.append((coef_north, pl.ds(2 * ROWS, SUBS), cols, jnp.where(sub < 4, 0.0, -twice_step * gravity * fm[1])))

        fm_s, cur_s, bef_s = row_pack(0, 0, j)
        for h in range(2):
            puts.append((coef_south, pl.ds(h * SUBS, SUBS), cols, twice_step * fm_s[h]))
            puts.append((coef_south, pl.ds(ROWS + h * SUBS, SUBS), cols, twice_step * cur_s[h]))
            puts.append((coef_south, pl.ds(2 * ROWS + h * SUBS, SUBS), cols, -twice_step * bef_s[h]))

        north_going, south_going = g + [s, m], cur_s + bef_s
        for q in range(4):
            puts.append((pay_a, pl.ds(q * SUBS, SUBS), cols, jnp.where(even, north_going[q], south_going[q])))
        into_b.append([jnp.where(even, jnp.where(lat == 0, 0.0, y), x) for x, y in zip(north_going, south_going)])
        turned = [jnp.take_along_axis(x, back, axis=1) for x in cur + bef]
        folded.append([x if q % 2 == 0 else -x for q, x in enumerate(turned)])
    for j in range(n_tiles):
        for q in range(4):
            value = jnp.where(is_top, folded[n_tiles - 1 - j][q], into_b[j][q])
            puts.append((pay_b, pl.ds((4 * j + q) * SUBS, SUBS), slice(None), value))
    for ref, rows, cols, value in puts:
        ref[rows, cols] = value


def inner_kernel(
    total_rows,
    raw_bef, raw_cur, scalar_flags, east_flags, north_flags,
    after_v, filtered_v,
    cur_v, bef_v, pres_v, flux_v,
):
    height, width = raw_cur.shape[2], raw_cur.shape[3]
    n_chunks, n_tiles = height // SUBS, width // LANES
    lat = lax.axis_index("lat")
    flags = (scalar_flags, east_flags, north_flags)

    zero = jnp.zeros((SUBS, LANES), jnp.float32)
    lane = lane_ids((SUBS, LANES))
    sub = row_ids((SUBS, LANES))
    first_lane, last_lane = lane == 0, lane == LANES - 1
    last_sub = sub == SUBS - 1
    tiles = [pl.ds(j * LANES, LANES) for j in range(n_tiles)]
    for l in range(LEVELS):
        for j in range(n_tiles):
            pres_v[l, j, pl.ds(height, SUBS), :] = zero
            for f in range(FIELDS):
                cur_v[f, l, j, pl.ds(height, SUBS), :] = zero
                bef_v[f, l, j, pl.ds(height, SUBS), :] = zero
                flux_v[f, l, j] = zero

    def store(puts):
        for ref, at, value in puts:
            ref[at] = value

    def each(op, *xs):
        return [op(*x) for x in zip(*xs)]

    def east_of(x):
        return [
            pltpu.roll(jnp.where(first_lane, b, a), LANES - 1, 1) for a, b in zip(x, x[1:] + [zero])
        ]

    def west_of(x):
        return [pltpu.roll(jnp.where(last_lane, b, a), 1, 1) for a, b in zip(x, [zero] + x[:-1])]

    def south_of(x, below):
        return [pltpu.roll(jnp.where(last_sub, b, a), 1, 0) for a, b in zip(x, below)]

    def face_flux(s, m, x, x_next, y, y_next):
        return each(lambda s, m, x, xn, y, yn: s * (x + xn) - m * (yn - y), s, m, x, x_next, y, y_next)

    def at(ref, r):
        return [ref[j, r, :] for j in range(n_tiles)]

    half = twice_step

    def unit(c, l, fields):
        rows = pl.ds(pl.multiple_of(c * SUBS, SUBS), SUBS)
        shifted = pl.ds(c * SUBS + 1, SUBS)

        def flag(t):
            return [flags[t][l, rows, cols].astype(jnp.float32) for cols in tiles]

        cur_e = {f: east_of(at(cur_v.at[f, l], rows)) for f in fields}
        bef_e = {f: east_of(at(bef_v.at[f, l], rows)) for f in fields}
        pres_e = east_of(at(pres_v.at[l], rows)) if 2 in fields else None
        yield []
        s_e, m_e = [half * speed_coef * x for x in at(cur_v.at[2, l], rows)], [half * diffuse_coef * x for x in flag(1)]
        s_n, m_n = [half * speed_coef * x for x in at(cur_v.at[3, l], rows)], [half * diffuse_coef * x for x in flag(2)]
        puts, own, west, south = [], {}, {}, {}
        for f in fields:
            cur, bef = at(cur_v.at[f, l], rows), at(bef_v.at[f, l], rows)
            flux_e = face_flux(s_e, m_e, cur, cur_e[f], bef, bef_e[f])
            flux_n = face_flux(s_n, m_n, cur, at(cur_v.at[f, l], shifted), bef, at(bef_v.at[f, l], shifted))
            west[f] = west_of(flux_e)
            south[f] = south_of(flux_n, at(flux_v.at[f, l], slice(None)))
            own[f] = each(lambda e, n: e + n, flux_e, flux_n)
            puts += [(flux_v, (f, l, j), x) for j, x in enumerate(flux_n)]
        yield puts
        puts = []
        for f in fields:
            cur, bef = at(cur_v.at[f, l], rows), at(bef_v.at[f, l], rows)
            mask = flag(mask_of(f))
            tend = each(lambda w, s, o: (w + s) - o, west[f], south[f], own[f])
            if f >= 2:
                index = (lat * height + c * SUBS + sub).astype(jnp.float32)
                cor = half * coriolis * (2.0 * (index + 0.5) / total_rows - 1.0)
                pres = at(pres_v.at[l], rows)
                ahead = pres_e if f == 2 else at(pres_v.at[l], shifted)
                slope = each(lambda m, a, p: (half * gravity) * m * (a - p), mask, ahead, pres)
                if f == 2:
                    tend = each(lambda t, v, g: t + (cor * v - g), tend, at(cur_v.at[3, l], rows), slope)
                else:
                    tend = each(lambda t, u, g: t - (cor * u + g), tend, at(cur_v.at[2, l], rows), slope)
            new = each(lambda b, t, m: (b + t) * m, bef, tend, mask)
            mid = each(lambda c, b, n: (1.0 - 2.0 * asselin) * c + asselin * (b + n), cur, bef, new)
            for cols, a, x in zip(tiles, new, mid):
                puts.append((after_v, (f, l, rows, cols), a))
                puts.append((filtered_v, (f, l, rows, cols), x))
        yield puts

    def masking(c):
        rows = pl.ds(pl.multiple_of(c * SUBS, SUBS), SUBS)
        totals = [zero] * n_tiles
        for l in range(LEVELS):
            for part in (range(0, n_tiles // 2), range(n_tiles // 2, n_tiles)):
                puts = []
                for j in part:
                    cols = tiles[j]
                    masks = [flags[t][l, rows, cols].astype(jnp.float32) for t in range(3)]
                    cur = [raw_cur[f, l, rows, cols] * masks[mask_of(f)] for f in range(FIELDS)]
                    rho = haline * cur[1] - thermal * cur[0]
                    totals[j] = totals[j] + rho
                    puts.append((pres_v, (l, j, rows), totals[j] - 0.5 * rho))
                    for f in range(FIELDS):
                        puts.append((cur_v, (f, l, j, rows), cur[f]))
                        puts.append((bef_v, (f, l, j, rows), raw_bef[f, l, rows, cols] * masks[mask_of(f)]))
                yield puts

    for c in range(2):
        for puts in masking(c):
            store(puts)

    def two_chunks(i, carry):
        units = [unit(2 * i + k, l, range(FIELDS)) for k in range(2) for l in range(LEVELS)]
        later = [masking(jnp.minimum(2 * i + 2 + k, n_chunks - 1)) for k in range(2)]
        per_chunk = len(units) // 2
        for t in range(len(units) + 2):
            puts = []
            for u in (t, t - 1, t - 2):
                if 0 <= u < len(units):
                    puts += next(units[u])
            if t < len(units):
                puts += next(later[t // per_chunk]) + next(later[t // per_chunk])
            store(puts)
        return carry

    lax.fori_loop(0, n_chunks // 2, two_chunks, 0)


def rim_kernel(
    got_a, got_b, got_east, got_west, coef_north, coef_south, coef_west, coef_east,
    after_v, filtered_v,
    after, filtered, after_w, filtered_w,
    add_rows, add_cols, sems,
):
    height, width = after.shape[2], after.shape[3]
    n_chunks, n_tiles = height // SUBS, width // LANES
    lane = lane_ids((SUBS, LANES))
    sub = row_ids((SUBS, LANES))
    even = lax.axis_index("lat") % 2 == 0

    def out(i, rows, cols):
        copies = [
            pltpu.make_async_copy(s.at[:, :, rows, cols], d.at[:, :, rows, cols], sems.at[i, q])
            for q, (s, d) in enumerate(((after_w, after), (filtered_w, filtered)))
        ]
        for copy in copies:
            copy.start()
        return copies

    middle = pl.ds(SUBS, height - 2 * SUBS)
    pending = out(2, middle, pl.ds(LANES, width - 2 * LANES))

    for j in range(n_tiles):
        cols = pl.ds(j * LANES, LANES)
        got = [(got_a[pl.ds(q * SUBS, SUBS), cols], got_b[pl.ds((4 * j + q) * SUBS, SUBS), :]) for q in range(4)]
        north = [jnp.where(even, a, b) for a, b in got]
        south = [jnp.where(even, b, a) for a, b in got]

        def coef(ref, q):
            return ref[pl.ds(q * SUBS, SUBS), cols]

        rho = jnp.where(sub < LEVELS, haline * pltpu.roll(north[0], LEVELS, 0) - thermal * north[0], 0.0)
        total = rho + pltpu.roll(rho, 1, 0)
        total = total + pltpu.roll(total, 2, 0)
        pres = pltpu.roll(total - 0.5 * rho, LEVELS, 0)
        for h in range(2):
            at = pl.ds(h * SUBS, SUBS)
            up = coef(coef_north, h) * north[h] + coef(coef_north, 2 + h) * north[2 + h]
            if h == 1:
                up = up + coef(coef_north, 4) * pres
            add_rows[1, at, cols] = up
            add_rows[0, at, cols] = (
                coef(coef_south, h) * south[h]
                + coef(coef_south, 2 + h) * south[2]
                + coef(coef_south, 4 + h) * south[3]
            )

    for side, (got, coef) in enumerate(((got_west[...], coef_west), (got_east[...], coef_east))):
        for part in range(2):
            rows = pl.ds(part * (height // 2), height // 2)
            x = got if part == 0 else pltpu.roll(got, LANES // 2, 1)
            x = x * coef[rows, :]
            add_cols[side, rows, :] = (
                x + pltpu.roll(x, LANES - ROWS, 1) + pltpu.roll(x, LANES - 2 * ROWS, 1)
            )

    def edge_cols(rows):
        return add_cols[0, rows, :], add_cols[1, rows, :]

    def put(value, k, at):
        return jnp.where(lane == at, jnp.broadcast_to(value[:, k : k + 1], (SUBS, LANES)), 0.0)

    def apply(extras):
        sums = [(at, after_v[at] + x, filtered_v[at] + asselin * x) for at, x in extras]
        for at, new, mid in sums:
            after_w[at] = new
            filtered_w[at] = mid

    def row_chunk(c, side, line):
        rows = pl.ds(c * SUBS, SUBS)
        west, east = edge_cols(rows)
        for f in range(FIELDS):
            extras = []
            for l in range(LEVELS):
                k = f * LEVELS + l
                for j in range(n_tiles):
                    cols = pl.ds(j * LANES, LANES)
                    extra = jnp.where(sub == line, jnp.broadcast_to(add_rows[side, pl.ds(k, 1), cols], (SUBS, LANES)), 0.0)
                    if j == 0:
                        extra = extra + put(west, k, 0)
                    if j == n_tiles - 1:
                        extra = extra + put(east, k, LANES - 1)
                    extras.append(((f, l, rows, cols), extra))
            apply(extras)

    def side_chunk(c):
        first, last = pl.ds(0, LANES), pl.ds(width - LANES, LANES)
        tiles = [pl.ds(pl.multiple_of(r * SUBS, SUBS), SUBS) for r in (c, c + 1)]
        edges = [edge_cols(rows) for rows in tiles]
        for f in range(FIELDS):
            extras = []
            for l in range(LEVELS):
                k = f * LEVELS + l
                for rows, (west, east) in zip(tiles, edges):
                    extras.append(((f, l, rows, first), put(west, k, 0)))
                    extras.append(((f, l, rows, last), put(east, k, LANES - 1)))
            apply(extras)

    row_chunk(0, 0, 0)
    pending += out(0, pl.ds(0, SUBS), pl.ds(0, width))
    row_chunk(n_chunks - 1, 1, SUBS - 1)
    pending += out(1, pl.ds(height - SUBS, SUBS), pl.ds(0, width))
    for c in range(1, n_chunks - 1, 2):
        side_chunk(c)
        rows = pl.ds(c * SUBS, 2 * SUBS)
        pending += out(2 + c, rows, pl.ds(0, LANES))
        pending += out(3 + c, rows, pl.ds(width - LANES, LANES))
    for copy in pending:
        copy.wait()


def shards(n_lat, earlier_state, present_state, scalar_wet_flags, eastside_wet_flags, northside_wet_flags):
    args = (earlier_state, present_state, scalar_wet_flags, eastside_wet_flags, northside_wet_flags)
    height, width = present_state.shape[2:]
    n_lon = lax.axis_size("lon")
    f32 = jnp.float32
    params = pltpu.CompilerParams(vmem_limit_bytes=VMEM_LIMIT)
    state = (FIELDS, LEVELS, height, width)
    apart = (LEVELS, width // LANES, height + SUBS, LANES)

    def vmem(*shape):
        return pltpu.VMEM(shape, f32)

    edges = pl.pallas_call(
        functools.partial(edges_kernel, n_lat),
        out_shape=[
            vmem(2 * ROWS, width), vmem(2 * ROWS * (width // LANES) + SUBS, LANES),
            vmem(height // 2, LANES), vmem(height // 2, LANES),
            vmem(2 * ROWS + SUBS, width), vmem(3 * ROWS, width), vmem(height, LANES), vmem(height, LANES),
        ],
        in_specs=[ANY] * 5,
        out_specs=[VMEM] * 8,
        scratch_shapes=[
            pltpu.VMEM((2, 2, FIELDS, LEVELS, height, LANES), f32),
            pltpu.VMEM((2, 3, LEVELS, height, LANES), jnp.int32),
            pltpu.VMEM((2, 2, FIELDS, LEVELS, SUBS, width), f32),
            pltpu.VMEM((2, 3, LEVELS, SUBS, width), jnp.int32),
            pltpu.SemaphoreType.DMA((20,)),
        ],
        compiler_params=params,
        cost_estimate=pl.CostEstimate(flops=500_000, bytes_accessed=3_600_000, transcendentals=0),
        name="edges",
    )(*[pltpu.with_memory_space_constraint(x, pltpu.HBM) for x in args])
    pay_a, pay_b, pay_west, pay_east, *coefs = edges

    def device(lon, lat):
        return lon * n_lat + lat

    lons, lats, top = range(n_lon), range(n_lat), n_lat - 1
    pairs_a = [(device(lon, lat), device(lon, lat ^ 1)) for lon in lons for lat in lats]
    pairs_b = [
        (
            device(lon, lat),
            device(n_lon - 1 - lon, lat) if lat in (0, top) else device(lon, lat + 1 if lat % 2 else lat - 1),
        )
        for lon in lons
        for lat in lats
    ]
    got_b = lax.ppermute(pay_b, ("lon", "lat"), pairs_b)
    got_a = lax.ppermute(pay_a, ("lon", "lat"), pairs_a)
    got_east = lax.ppermute(pay_west, "lon", [(i, (i - 1) % n_lon) for i in lons])
    got_west = lax.ppermute(pay_east, "lon", [(i, (i + 1) % n_lon) for i in lons])

    after_v, filtered_v = pl.pallas_call(
        functools.partial(inner_kernel, height * n_lat),
        out_shape=[vmem(*state), vmem(*state)],
        in_specs=[VMEM] * 5,
        out_specs=[VMEM, VMEM],
        scratch_shapes=[
            pltpu.VMEM((FIELDS, *apart), f32),
            pltpu.VMEM((FIELDS, *apart), f32),
            pltpu.VMEM(apart, f32),
            pltpu.VMEM((FIELDS, LEVELS, width // LANES, SUBS, LANES), f32),
        ],
        compiler_params=params,
        cost_estimate=pl.CostEstimate(flops=20_000_000, bytes_accessed=9_000_000, transcendentals=0),
        name="inner",
    )(*[pltpu.with_memory_space_constraint(x, pltpu.VMEM) for x in args])

    def in_vmem(x):
        return pltpu.with_memory_space_constraint(x, pltpu.VMEM)

    fixed = [in_vmem(x) for x in (got_a, got_b, got_east, got_west, *coefs, after_v, filtered_v)]
    after, filtered, _, _ = pl.pallas_call(
        rim_kernel,
        out_shape=[pltpu.HBM(state, f32), pltpu.HBM(state, f32), vmem(*state), vmem(*state)],
        in_specs=[VMEM] * 10,
        out_specs=[ANY, ANY, VMEM, VMEM],
        scratch_shapes=[
            pltpu.VMEM((2, ROWS, width), f32),
            pltpu.VMEM((2, height, LANES), f32),
            pltpu.SemaphoreType.DMA((3 + height // SUBS, 2)),
        ],
        input_output_aliases={8: 2, 9: 3},
        compiler_params=params,
        cost_estimate=pl.CostEstimate(flops=500_000, bytes_accessed=3_000_000, transcendentals=0),
        name="rim",
    )(*fixed)
    return after, filtered


def solution(mesh):
    placed = (
        P(None, None, "lat", "lon"),
        P(None, None, "lat", "lon"),
        P(None, "lat", "lon"),
        P(None, "lat", "lon"),
        P(None, "lat", "lon"),
    )
    return jax.shard_map(
        functools.partial(shards, mesh.shape["lat"]),
        mesh=mesh,
        in_specs=placed,
        out_specs=(P(None, None, "lat", "lon"), P(None, None, "lat", "lon")),
        check_vma=False,
    )
```

```python
import functools

import jax
import jax.numpy as jnp
from jax import lax
from jax.experimental import pallas as pl
from jax.experimental.pallas import tpu as pltpu
from jax.sharding import PartitionSpec as P

advect_coef = 0.5
diffuse_coef = 0.25
twice_step = 0.5
gravity = 0.5
coriolis = 0.5
thermal = 0.2
haline = 0.15
asselin = 0.1

LANES = 128
SUBS = 8
FIELDS = 4
LEVELS = 4
ROWS = FIELDS * LEVELS
VMEM_LIMIT = 24 * 1024 * 1024

speed_coef = advect_coef * 0.5
ANY = pl.BlockSpec(memory_space=pl.ANY)
VMEM = pl.BlockSpec(memory_space=pltpu.VMEM)


def mask_of(field):
    return max(field - 1, 0)


def lane_ids(shape):
    return lax.broadcasted_iota(jnp.int32, shape, len(shape) - 1)


def row_ids(shape):
    return lax.broadcasted_iota(jnp.int32, shape, len(shape) - 2)


def edges_kernel(
    n_lat,
    earlier, present, scalar_flags, east_flags, north_flags,
    pay_a, pay_b, pay_west, pay_east, coef_north, coef_south, coef_west, coef_east,
    col_state, col_flag, row_state, row_flag, sems,
):
    height, width = present.shape[2], present.shape[3]
    lat = lax.axis_index("lat")
    flags = (scalar_flags, east_flags, north_flags)
    copies = []
    for side in range(2):
        cols = pl.ds(0 if side == 0 else width - LANES, LANES)
        for t, state in enumerate((present, earlier)):
            copies.append((state.at[:, :, :, cols], col_state.at[side, t]))
        for t, flag in enumerate(flags):
            copies.append((flag.at[:, :, cols], col_flag.at[side, t]))
    for side in range(2):
        rows = pl.ds(0 if side == 0 else height - SUBS, SUBS)
        for t, state in enumerate((present, earlier)):
            copies.append((state.at[:, :, rows, :], row_state.at[side, t]))
        for t, flag in enumerate(flags):
            copies.append((flag.at[:, rows, :], row_flag.at[side, t]))
    copies = [
        pltpu.make_async_copy(src, dst, sems.at[i]) for i, (src, dst) in enumerate(copies)
    ]
    for copy in copies:
        copy.start()
    n_tiles = width // LANES
    lane = lane_ids((SUBS, LANES))
    sub = row_ids((SUBS, LANES))

    for copy in copies[:10]:
        copy.wait()

    base, level = lane & (ROWS - 1), lane & (LEVELS - 1)
    zeros = jnp.zeros((SUBS, LANES), jnp.float32)
    tiles = range(height // SUBS)

    def columns(x, at):
        return [jnp.broadcast_to(x[r * SUBS : (r + 1) * SUBS, at : at + 1], (SUBS, LANES)) for r in tiles]

    def placed(where, xs, old):
        return [jnp.where(where, x, o) for x, o in zip(xs, old)]

    def col_pack(side, at):
        fm, both, extra, u, total = ([zeros] * len(tiles) for _ in range(5))
        for l in range(LEVELS):
            mask = [columns(col_flag[side, t, l].astype(jnp.float32), at) for t in range(3)]
            for f in range(FIELDS):
                fm = placed(base == f * LEVELS + l, mask[mask_of(f)], fm)
            now = []
            for f in range(FIELDS):
                now.append(columns(col_state[side, 0, f, l], at))
                both = placed(lane == f * LEVELS + l, now[f], both)
                both = placed(lane == ROWS + f * LEVELS + l, columns(col_state[side, 1, f, l], at), both)
            if side == 0:
                rho = [(haline * s - thermal * t) * m for s, t, m in zip(now[1], now[0], mask[0])]
                total = [a + b for a, b in zip(total, rho)]
                pres = [a - 0.5 * b for a, b in zip(total, rho)]
                extra = placed(lane == 2 * ROWS + 2 * LEVELS + l, pres, extra)
            else:
                extra = placed(level == l, mask[1], extra)
                u = placed(level == l, now[2], u)
        return zip(fm, both, extra, u)

    in_pres = (lane >= 2 * ROWS + 2 * LEVELS) & (lane < 2 * ROWS + 3 * LEVELS)
    going_west, going_east, coefs_west, coefs_east = [], [], [], []
    for fm, both, pres, _ in col_pack(0, 0):
        both = both * fm
        moved = pltpu.roll(both, ROWS, 1)
        going_west.append(both + pres)
        coefs_west.append(twice_step * jnp.where(lane < ROWS, fm, jnp.where(lane < 2 * ROWS, moved, -moved)))
    for fm, both, mu, u in col_pack(1, LANES - 1):
        s, dm = speed_coef * u * mu, diffuse_coef * mu
        own = both * fm * jnp.where(lane < ROWS, s, dm)
        g = own + pltpu.roll(own, LANES - ROWS, 1)
        going_east.append(jnp.where(lane < ROWS, g, jnp.where(lane < 2 * ROWS, s, dm)))
        face = jnp.where(lane < ROWS, -twice_step * s, twice_step * dm) * fm
        coefs_east.append(
            jnp.where(lane < 2 * ROWS, face, jnp.where(in_pres, -twice_step * gravity * mu, 0.0))
        )
    half = len(tiles) // 2
    folded = [
        [jnp.where(lane < LANES // 2, x[r], pltpu.roll(x[r + half], LANES // 2, 1)) for r in range(half)]
        for x in (going_west, going_east)
    ]
    for r in tiles:
        rows = pl.ds(r * SUBS, SUBS)
        coef_west[rows, :] = coefs_west[r]
        coef_east[rows, :] = coefs_east[r]
        if r < half:
            pay_west[rows, :] = folded[0][r]
            pay_east[rows, :] = folded[1][r]

    for copy in copies[10:]:
        copy.wait()

    def row_pack(side, at, j):
        line = pl.ds(at, 1)
        cols = pl.ds(j * LANES, LANES)

        def gather(rows):
            packed = jnp.broadcast_to(rows[0], (SUBS, LANES))
            for k in range(1, SUBS):
                packed = jnp.where(sub == k, jnp.broadcast_to(rows[k], (SUBS, LANES)), packed)
            return packed

        def flag_row(t, l):
            return row_flag[side, t, l, line, cols].astype(jnp.float32)

        fm = [
            gather([flag_row(mask_of(f), l) for f in (2 * h, 2 * h + 1) for l in range(LEVELS)])
            for h in range(2)
        ]
        cur, bef = (
            [
                fm[h]
                * gather([row_state[side, t, f, l, line, cols] for f in (2 * h, 2 * h + 1) for l in range(LEVELS)])
                for h in range(2)
            ]
            for t in range(2)
        )
        return fm, cur, bef

    back = LANES - 1 - lane
    even = lat % 2 == 0
    is_top = lat == n_lat - 1
    puts = [
        (ref, pl.ds(r, SUBS), slice(None), zeros)
        for ref, used in ((pay_b, 2 * ROWS * n_tiles), (pay_west, height // 2), (pay_east, height // 2))
        for r in range(used, ref.shape[0], SUBS)
    ]
    into_b, folded = [], []
    for j in range(n_tiles):
        cols = pl.ds(j * LANES, LANES)
        fm, cur, bef = row_pack(1, SUBS - 1, j)
        s = speed_coef * jnp.where(sub < 4, pltpu.roll(cur[1], 4, 0), cur[1])
        m = diffuse_coef * jnp.where(sub < 4, pltpu.roll(fm[1], 4, 0), fm[1])
        g = [s * cur[h] + m * bef[h] for h in range(2)]
        for h in range(2):
            puts.append((coef_north, pl.ds(h * SUBS, SUBS), cols, -twice_step * fm[h] * s))
            puts.append((coef_north, pl.ds(ROWS + h * SUBS, SUBS), cols, twice_step * fm[h] * m))
        puts.append((coef_north, pl.ds(2 * ROWS, SUBS), cols, jnp.where(sub < 4, 0.0, -twice_step * gravity * fm[1])))

        fm_s, cur_s, bef_s = row_pack(0, 0, j)
        for h in range(2):
            puts.append((coef_south, pl.ds(h * SUBS, SUBS), cols, twice_step * fm_s[h]))
            puts.append((coef_south, pl.ds(ROWS + h * SUBS, SUBS), cols, twice_step * cur_s[h]))
            puts.append((coef_south, pl.ds(2 * ROWS + h * SUBS, SUBS), cols, -twice_step * bef_s[h]))

        north_going, south_going = g + [s, m], cur_s + bef_s
        for q in range(4):
            puts.append((pay_a, pl.ds(q * SUBS, SUBS), cols, jnp.where(even, north_going[q], south_going[q])))
        into_b.append([jnp.where(even, jnp.where(lat == 0, 0.0, y), x) for x, y in zip(north_going, south_going)])
        turned = [jnp.take_along_axis(x, back, axis=1) for x in cur + bef]
        folded.append([x if q % 2 == 0 else -x for q, x in enumerate(turned)])
    for j in range(n_tiles):
        for q in range(4):
            value = jnp.where(is_top, folded[n_tiles - 1 - j][q], into_b[j][q])
            puts.append((pay_b, pl.ds((4 * j + q) * SUBS, SUBS), slice(None), value))
    for ref, rows, cols, value in puts:
        ref[rows, cols] = value


def inner_kernel(
    total_rows,
    raw_bef, raw_cur, scalar_flags, east_flags, north_flags,
    after_v, filtered_v,
    cur_v, bef_v, pres_v, flux_v,
):
    height, width = raw_cur.shape[2], raw_cur.shape[3]
    n_chunks, n_tiles = height // SUBS, width // LANES
    lat = lax.axis_index("lat")
    flags = (scalar_flags, east_flags, north_flags)

    zero = jnp.zeros((SUBS, LANES), jnp.float32)
    lane = lane_ids((SUBS, LANES))
    sub = row_ids((SUBS, LANES))
    first_lane, last_lane = lane == 0, lane == LANES - 1
    last_sub = sub == SUBS - 1
    tiles = [pl.ds(j * LANES, LANES) for j in range(n_tiles)]
    for l in range(LEVELS):
        for j in range(n_tiles):
            pres_v[l, j, pl.ds(height, SUBS), :] = zero
            for f in range(FIELDS):
                cur_v[f, l, j, pl.ds(height, SUBS), :] = zero
                bef_v[f, l, j, pl.ds(height, SUBS), :] = zero
                flux_v[f, l, j] = zero

    def store(puts):
        for ref, at, value in puts:
            ref[at] = value

    def each(op, *xs):
        return [op(*x) for x in zip(*xs)]

    def east_of(x):
        return [
            pltpu.roll(jnp.where(first_lane, b, a), LANES - 1, 1) for a, b in zip(x, x[1:] + [zero])
        ]

    def west_of(x):
        return [pltpu.roll(jnp.where(last_lane, b, a), 1, 1) for a, b in zip(x, [zero] + x[:-1])]

    def south_of(x, below):
        return [pltpu.roll(jnp.where(last_sub, b, a), 1, 0) for a, b in zip(x, below)]

    def face_flux(s, m, x, x_next, y, y_next):
        return each(lambda s, m, x, xn, y, yn: s * (x + xn) - m * (yn - y), s, m, x, x_next, y, y_next)

    def at(ref, r):
        return [ref[j, r, :] for j in range(n_tiles)]

    half = twice_step

    def unit(c, l, fields):
        rows = pl.ds(pl.multiple_of(c * SUBS, SUBS), SUBS)
        shifted = pl.ds(c * SUBS + 1, SUBS)

        def flag(t):
            return [flags[t][l, rows, cols].astype(jnp.float32) for cols in tiles]

        cur_e = {f: east_of(at(cur_v.at[f, l], rows)) for f in fields}
        bef_e = {f: east_of(at(bef_v.at[f, l], rows)) for f in fields}
        pres_e = east_of(at(pres_v.at[l], rows)) if 2 in fields else None
        yield []
        s_e, m_e = [half * speed_coef * x for x in at(cur_v.at[2, l], rows)], [half * diffuse_coef * x for x in flag(1)]
        s_n, m_n = [half * speed_coef * x for x in at(cur_v.at[3, l], rows)], [half * diffuse_coef * x for x in flag(2)]
        puts, own, west, south = [], {}, {}, {}
        for f in fields:
            cur, bef = at(cur_v.at[f, l], rows), at(bef_v.at[f, l], rows)
            flux_e = face_flux(s_e, m_e, cur, cur_e[f], bef, bef_e[f])
            flux_n = face_flux(s_n, m_n, cur, at(cur_v.at[f, l], shifted), bef, at(bef_v.at[f, l], shifted))
            west[f] = west_of(flux_e)
            south[f] = south_of(flux_n, at(flux_v.at[f, l], slice(None)))
            own[f] = each(lambda e, n: e + n, flux_e, flux_n)
            puts += [(flux_v, (f, l, j), x) for j, x in enumerate(flux_n)]
        yield puts
        puts = []
        for f in fields:
            cur, bef = at(cur_v.at[f, l], rows), at(bef_v.at[f, l], rows)
            mask = flag(mask_of(f))
            tend = each(lambda w, s, o: (w + s) - o, west[f], south[f], own[f])
            if f >= 2:
                index = (lat * height + c * SUBS + sub).astype(jnp.float32)
                cor = half * coriolis * (2.0 * (index + 0.5) / total_rows - 1.0)
                pres = at(pres_v.at[l], rows)
                ahead = pres_e if f == 2 else at(pres_v.at[l], shifted)
                slope = each(lambda m, a, p: (half * gravity) * m * (a - p), mask, ahead, pres)
                if f == 2:
                    tend = each(lambda t, v, g: t + (cor * v - g), tend, at(cur_v.at[3, l], rows), slope)
                else:
                    tend = each(lambda t, u, g: t - (cor * u + g), tend, at(cur_v.at[2, l], rows), slope)
            new = each(lambda b, t, m: (b + t) * m, bef, tend, mask)
            mid = each(lambda c, b, n: (1.0 - 2.0 * asselin) * c + asselin * (b + n), cur, bef, new)
            for cols, a, x in zip(tiles, new, mid):
                puts.append((after_v, (f, l, rows, cols), a))
                puts.append((filtered_v, (f, l, rows, cols), x))
        yield puts

    def masking(c):
        rows = pl.ds(pl.multiple_of(c * SUBS, SUBS), SUBS)
        totals = [zero] * n_tiles
        for l in range(LEVELS):
            for part in (range(0, n_tiles // 2), range(n_tiles // 2, n_tiles)):
                puts = []
                for j in part:
                    cols = tiles[j]
                    masks = [flags[t][l, rows, cols].astype(jnp.float32) for t in range(3)]
                    cur = [raw_cur[f, l, rows, cols] * masks[mask_of(f)] for f in range(FIELDS)]
                    rho = haline * cur[1] - thermal * cur[0]
                    totals[j] = totals[j] + rho
                    puts.append((pres_v, (l, j, rows), totals[j] - 0.5 * rho))
                    for f in range(FIELDS):
                        puts.append((cur_v, (f, l, j, rows), cur[f]))
                        puts.append((bef_v, (f, l, j, rows), raw_bef[f, l, rows, cols] * masks[mask_of(f)]))
                yield puts

    for puts in masking(0):
        store(puts)

    chunks = 4 if n_chunks % 4 == 0 else 1

    def some_chunks(i, carry):
        units = [unit(chunks * i + k, l, range(FIELDS)) for k in range(chunks) for l in range(LEVELS)]
        later = [masking(jnp.minimum(chunks * i + k + 1, n_chunks - 1)) for k in range(chunks)]
        for t in range(len(units) + 2):
            puts = []
            for u in (t, t - 1, t - 2):
                if 0 <= u < len(units):
                    puts += next(units[u])
            if t < len(units):
                puts += next(later[t // LEVELS]) + next(later[t // LEVELS])
            store(puts)
        return carry

    lax.fori_loop(0, n_chunks // chunks, some_chunks, 0)


def rim_kernel(
    got_a, got_b, got_east, got_west, coef_north, coef_south, coef_west, coef_east,
    after_v, filtered_v,
    after, filtered, after_w, filtered_w,
    add_rows, add_cols, sems,
):
    height, width = after.shape[2], after.shape[3]
    n_chunks, n_tiles = height // SUBS, width // LANES
    lane = lane_ids((SUBS, LANES))
    sub = row_ids((SUBS, LANES))
    even = lax.axis_index("lat") % 2 == 0

    def out(i, rows, cols):
        copies = [
            pltpu.make_async_copy(s.at[:, :, rows, cols], d.at[:, :, rows, cols], sems.at[i, q])
            for q, (s, d) in enumerate(((after_w, after), (filtered_w, filtered)))
        ]
        for copy in copies:
            copy.start()
        return copies

    middle = pl.ds(SUBS, height - 2 * SUBS)
    pending = out(2, middle, pl.ds(LANES, width - 2 * LANES))

    for j in range(n_tiles):
        cols = pl.ds(j * LANES, LANES)
        got = [(got_a[pl.ds(q * SUBS, SUBS), cols], got_b[pl.ds((4 * j + q) * SUBS, SUBS), :]) for q in range(4)]
        north = [jnp.where(even, a, b) for a, b in got]
        south = [jnp.where(even, b, a) for a, b in got]

        def coef(ref, q):
            return ref[pl.ds(q * SUBS, SUBS), cols]

        rho = jnp.where(sub < LEVELS, haline * pltpu.roll(north[0], LEVELS, 0) - thermal * north[0], 0.0)
        total = rho + pltpu.roll(rho, 1, 0)
        total = total + pltpu.roll(total, 2, 0)
        pres = pltpu.roll(total - 0.5 * rho, LEVELS, 0)
        for h in range(2):
            at = pl.ds(h * SUBS, SUBS)
            up = coef(coef_north, h) * north[h] + coef(coef_north, 2 + h) * north[2 + h]
            if h == 1:
                up = up + coef(coef_north, 4) * pres
            add_rows[1, at, cols] = up
            add_rows[0, at, cols] = (
                coef(coef_south, h) * south[h]
                + coef(coef_south, 2 + h) * south[2]
                + coef(coef_south, 4 + h) * south[3]
            )

    for side, (got, coef) in enumerate(((got_west[pl.ds(0, height // 2), :], coef_west), (got_east[pl.ds(0, height // 2), :], coef_east))):
        for part in range(2):
            rows = pl.ds(part * (height // 2), height // 2)
            x = got if part == 0 else pltpu.roll(got, LANES // 2, 1)
            x = x * coef[rows, :]
            add_cols[side, rows, :] = (
                x + pltpu.roll(x, LANES - ROWS, 1) + pltpu.roll(x, LANES - 2 * ROWS, 1)
            )

    def edge_cols(rows):
        return add_cols[0, rows, :], add_cols[1, rows, :]

    def put(value, k, at):
        return jnp.where(lane == at, jnp.broadcast_to(value[:, k : k + 1], (SUBS, LANES)), 0.0)

    def apply(extras):
        sums = [(at, after_v[at] + x, filtered_v[at] + asselin * x) for at, x in extras]
        for at, new, mid in sums:
            after_w[at] = new
            filtered_w[at] = mid

    def row_chunk(c, side, line):
        rows = pl.ds(c * SUBS, SUBS)
        west, east = edge_cols(rows)
        for f in range(FIELDS):
            extras = []
            for l in range(LEVELS):
                k = f * LEVELS + l
                for j in range(n_tiles):
                    cols = pl.ds(j * LANES, LANES)
                    extra = jnp.where(sub == line, jnp.broadcast_to(add_rows[side, pl.ds(k, 1), cols], (SUBS, LANES)), 0.0)
                    if j == 0:
                        extra = extra + put(west, k, 0)
                    if j == n_tiles - 1:
                        extra = extra + put(east, k, LANES - 1)
                    extras.append(((f, l, rows, cols), extra))
            apply(extras)

    def side_chunk(c):
        first, last = pl.ds(0, LANES), pl.ds(width - LANES, LANES)
        tiles = [pl.ds(pl.multiple_of(r * SUBS, SUBS), SUBS) for r in (c, c + 1)]
        edges = [edge_cols(rows) for rows in tiles]
        for f in range(FIELDS):
            extras = []
            for l in range(LEVELS):
                k = f * LEVELS + l
                for rows, (west, east) in zip(tiles, edges):
                    extras.append(((f, l, rows, first), put(west, k, 0)))
                    extras.append(((f, l, rows, last), put(east, k, LANES - 1)))
            apply(extras)

    row_chunk(0, 0, 0)
    pending += out(0, pl.ds(0, SUBS), pl.ds(0, width))
    row_chunk(n_chunks - 1, 1, SUBS - 1)
    pending += out(1, pl.ds(height - SUBS, SUBS), pl.ds(0, width))
    for c in range(1, n_chunks - 1, 2):
        side_chunk(c)
        rows = pl.ds(c * SUBS, 2 * SUBS)
        pending += out(2 + c, rows, pl.ds(0, LANES))
        pending += out(3 + c, rows, pl.ds(width - LANES, LANES))
    for copy in pending:
        copy.wait()


def shards(n_lat, earlier_state, present_state, scalar_wet_flags, eastside_wet_flags, northside_wet_flags):
    args = (earlier_state, present_state, scalar_wet_flags, eastside_wet_flags, northside_wet_flags)
    height, width = present_state.shape[2:]
    n_lon = lax.axis_size("lon")
    f32 = jnp.float32
    params = pltpu.CompilerParams(vmem_limit_bytes=VMEM_LIMIT)
    state = (FIELDS, LEVELS, height, width)
    apart = (LEVELS, width // LANES, height + SUBS, LANES)

    wide = 2 * ROWS * (width // LANES)

    def vmem(*shape):
        return pltpu.VMEM(shape, f32)

    edges = pl.pallas_call(
        functools.partial(edges_kernel, n_lat),
        out_shape=[
            vmem(2 * ROWS, width), vmem(wide + 2 * SUBS, LANES),
            vmem(max(wide + SUBS, height // 2), LANES), vmem(max(wide + SUBS, height // 2), LANES),
            vmem(2 * ROWS + SUBS, width), vmem(3 * ROWS, width), vmem(height, LANES), vmem(height, LANES),
        ],
        in_specs=[ANY] * 5,
        out_specs=[VMEM] * 8,
        scratch_shapes=[
            pltpu.VMEM((2, 2, FIELDS, LEVELS, height, LANES), f32),
            pltpu.VMEM((2, 3, LEVELS, height, LANES), jnp.int32),
            pltpu.VMEM((2, 2, FIELDS, LEVELS, SUBS, width), f32),
            pltpu.VMEM((2, 3, LEVELS, SUBS, width), jnp.int32),
            pltpu.SemaphoreType.DMA((20,)),
        ],
        compiler_params=params,
        cost_estimate=pl.CostEstimate(flops=500_000, bytes_accessed=3_600_000, transcendentals=0),
        name="edges",
    )(*[pltpu.with_memory_space_constraint(x, pltpu.HBM) for x in args])
    pay_a, pay_b, pay_west, pay_east, *coefs = edges

    def device(lon, lat):
        return lon * n_lat + lat

    lons, lats, top = range(n_lon), range(n_lat), n_lat - 1
    pairs_a = [(device(lon, lat), device(lon, lat ^ 1)) for lon in lons for lat in lats]
    pairs_b = [
        (
            device(lon, lat),
            device(n_lon - 1 - lon, lat) if lat in (0, top) else device(lon, lat + 1 if lat % 2 else lat - 1),
        )
        for lon in lons
        for lat in lats
    ]
    got_b = lax.ppermute(pay_b, ("lon", "lat"), pairs_b)
    got_a = lax.ppermute(pay_a, ("lon", "lat"), pairs_a)
    got_east = lax.ppermute(pay_west, "lon", [(i, (i - 1) % n_lon) for i in lons])
    got_west = lax.ppermute(pay_east, "lon", [(i, (i + 1) % n_lon) for i in lons])

    after_v, filtered_v = pl.pallas_call(
        functools.partial(inner_kernel, height * n_lat),
        out_shape=[vmem(*state), vmem(*state)],
        in_specs=[VMEM] * 5,
        out_specs=[VMEM, VMEM],
        scratch_shapes=[
            pltpu.VMEM((FIELDS, *apart), f32),
            pltpu.VMEM((FIELDS, *apart), f32),
            pltpu.VMEM(apart, f32),
            pltpu.VMEM((FIELDS, LEVELS, width // LANES, SUBS, LANES), f32),
        ],
        compiler_params=params,
        cost_estimate=pl.CostEstimate(flops=20_000_000, bytes_accessed=9_000_000, transcendentals=0),
        name="inner",
    )(*[pltpu.with_memory_space_constraint(x, pltpu.VMEM) for x in args])

    def in_vmem(x):
        return pltpu.with_memory_space_constraint(x, pltpu.VMEM)

    fixed = [in_vmem(x) for x in (got_a, got_b, got_east, got_west, *coefs, after_v, filtered_v)]
    after, filtered, _, _ = pl.pallas_call(
        rim_kernel,
        out_shape=[pltpu.HBM(state, f32), pltpu.HBM(state, f32), vmem(*state), vmem(*state)],
        in_specs=[VMEM] * 10,
        out_specs=[ANY, ANY, VMEM, VMEM],
        scratch_shapes=[
            pltpu.VMEM((2, ROWS, width), f32),
            pltpu.VMEM((2, height, LANES), f32),
            pltpu.SemaphoreType.DMA((3 + height // SUBS, 2)),
        ],
        input_output_aliases={8: 2, 9: 3},
        compiler_params=params,
        cost_estimate=pl.CostEstimate(flops=500_000, bytes_accessed=3_000_000, transcendentals=0),
        name="rim",
    )(*fixed)
    return after, filtered


def solution(mesh):
    placed = (
        P(None, None, "lat", "lon"),
        P(None, None, "lat", "lon"),
        P(None, "lat", "lon"),
        P(None, "lat", "lon"),
        P(None, "lat", "lon"),
    )
    return jax.shard_map(
        functools.partial(shards, mesh.shape["lat"]),
        mesh=mesh,
        in_specs=placed,
        out_specs=(P(None, None, "lat", "lon"), P(None, None, "lat", "lon")),
        check_vma=False,
    )
```

```python
import functools

import jax
import jax.numpy as jnp
from jax import lax
from jax.experimental import pallas as pl
from jax.experimental.pallas import tpu as pltpu
from jax.sharding import PartitionSpec as P

advect_coef = 0.5
diffuse_coef = 0.25
twice_step = 0.5
gravity = 0.5
coriolis = 0.5
thermal = 0.2
haline = 0.15
asselin = 0.1

LANES = 128
SUBS = 8
FIELDS = 4
LEVELS = 4
ROWS = FIELDS * LEVELS
VMEM_LIMIT = 24 * 1024 * 1024

speed_coef = advect_coef * 0.5
ANY = pl.BlockSpec(memory_space=pl.ANY)
VMEM = pl.BlockSpec(memory_space=pltpu.VMEM)


def mask_of(field):
    return max(field - 1, 0)


def lane_ids(shape):
    return lax.broadcasted_iota(jnp.int32, shape, len(shape) - 1)


def row_ids(shape):
    return lax.broadcasted_iota(jnp.int32, shape, len(shape) - 2)


def edges_kernel(
    n_lat,
    earlier, present, scalar_flags, east_flags, north_flags,
    pay_a, pay_b, pay_west, pay_east, coef_north, coef_south, coef_west, coef_east,
    col_state, col_flag, row_state, row_flag, sems,
):
    height, width = present.shape[2], present.shape[3]
    lat = lax.axis_index("lat")
    flags = (scalar_flags, east_flags, north_flags)
    copies = []
    for side in range(2):
        cols = pl.ds(0 if side == 0 else width - LANES, LANES)
        for t, state in enumerate((present, earlier)):
            copies.append((state.at[:, :, :, cols], col_state.at[side, t]))
        for t, flag in enumerate(flags):
            copies.append((flag.at[:, :, cols], col_flag.at[side, t]))
    for side in range(2):
        rows = pl.ds(0 if side == 0 else height - SUBS, SUBS)
        for t, state in enumerate((present, earlier)):
            copies.append((state.at[:, :, rows, :], row_state.at[side, t]))
        for t, flag in enumerate(flags):
            copies.append((flag.at[:, rows, :], row_flag.at[side, t]))
    copies = [
        pltpu.make_async_copy(src, dst, sems.at[i]) for i, (src, dst) in enumerate(copies)
    ]
    for copy in copies:
        copy.start()
    n_tiles = width // LANES
    lane = lane_ids((SUBS, LANES))
    sub = row_ids((SUBS, LANES))

    for copy in copies[:5]:
        copy.wait()

    base, level = lane & (ROWS - 1), lane & (LEVELS - 1)
    zeros = jnp.zeros((SUBS, LANES), jnp.float32)
    tiles = range(height // SUBS)

    def columns(x, at):
        return [jnp.broadcast_to(x[r * SUBS : (r + 1) * SUBS, at : at + 1], (SUBS, LANES)) for r in tiles]

    def placed(where, xs, old):
        return [jnp.where(where, x, o) for x, o in zip(xs, old)]

    def col_pack(side, at):
        fm, both, extra, u, total = ([zeros] * len(tiles) for _ in range(5))
        for l in range(LEVELS):
            mask = [columns(col_flag[side, t, l].astype(jnp.float32), at) for t in range(3)]
            for f in range(FIELDS):
                fm = placed(base == f * LEVELS + l, mask[mask_of(f)], fm)
            now = []
            for f in range(FIELDS):
                now.append(columns(col_state[side, 0, f, l], at))
                both = placed(lane == f * LEVELS + l, now[f], both)
                both = placed(lane == ROWS + f * LEVELS + l, columns(col_state[side, 1, f, l], at), both)
            if side == 0:
                rho = [(haline * s - thermal * t) * m for s, t, m in zip(now[1], now[0], mask[0])]
                total = [a + b for a, b in zip(total, rho)]
                pres = [a - 0.5 * b for a, b in zip(total, rho)]
                extra = placed(lane == 2 * ROWS + 2 * LEVELS + l, pres, extra)
            else:
                extra = placed(level == l, mask[1], extra)
                u = placed(level == l, now[2], u)
        return zip(fm, both, extra, u)

    in_pres = (lane >= 2 * ROWS + 2 * LEVELS) & (lane < 2 * ROWS + 3 * LEVELS)
    going_west, going_east, coefs_west, coefs_east = [], [], [], []

    def put_column(pay, coef, going, coefs):
        half = len(tiles) // 2
        folded = [jnp.where(lane < LANES // 2, going[r], pltpu.roll(going[r + half], LANES // 2, 1)) for r in range(half)]
        for r in tiles:
            coef[pl.ds(r * SUBS, SUBS), :] = coefs[r]
            if r < half:
                pay[pl.ds(r * SUBS, SUBS), :] = folded[r]

    for fm, both, pres, _ in col_pack(0, 0):
        both = both * fm
        moved = pltpu.roll(both, ROWS, 1)
        going_west.append(both + pres)
        coefs_west.append(twice_step * jnp.where(lane < ROWS, fm, jnp.where(lane < 2 * ROWS, moved, -moved)))
    put_column(pay_west, coef_west, going_west, coefs_west)
    for copy in copies[5:10]:
        copy.wait()
    for fm, both, mu, u in col_pack(1, LANES - 1):
        s, dm = speed_coef * u * mu, diffuse_coef * mu
        own = both * fm * jnp.where(lane < ROWS, s, dm)
        g = own + pltpu.roll(own, LANES - ROWS, 1)
        going_east.append(jnp.where(lane < ROWS, g, jnp.where(lane < 2 * ROWS, s, dm)))
        face = jnp.where(lane < ROWS, -twice_step * s, twice_step * dm) * fm
        coefs_east.append(
            jnp.where(lane < 2 * ROWS, face, jnp.where(in_pres, -twice_step * gravity * mu, 0.0))
        )
    put_column(pay_east, coef_east, going_east, coefs_east)
    for copy in copies[10:]:
        copy.wait()

    def row_pack(side, at, j):
        line = pl.ds(at, 1)
        cols = pl.ds(j * LANES, LANES)

        def gather(rows):
            packed = jnp.broadcast_to(rows[0], (SUBS, LANES))
            for k in range(1, SUBS):
                packed = jnp.where(sub == k, jnp.broadcast_to(rows[k], (SUBS, LANES)), packed)
            return packed

        def flag_row(t, l):
            return row_flag[side, t, l, line, cols].astype(jnp.float32)

        fm = [
            gather([flag_row(mask_of(f), l) for f in (2 * h, 2 * h + 1) for l in range(LEVELS)])
            for h in range(2)
        ]
        cur, bef = (
            [
                fm[h]
                * gather([row_state[side, t, f, l, line, cols] for f in (2 * h, 2 * h + 1) for l in range(LEVELS)])
                for h in range(2)
            ]
            for t in range(2)
        )
        return fm, cur, bef

    back = LANES - 1 - lane
    even = lat % 2 == 0
    is_top = lat == n_lat - 1
    puts = [
        (ref, pl.ds(r, SUBS), slice(None), zeros)
        for ref, used in ((pay_b, 2 * ROWS * n_tiles), (pay_west, height // 2), (pay_east, height // 2))
        for r in range(used, ref.shape[0], SUBS)
    ]
    into_b, folded = [], []
    for j in range(n_tiles):
        cols = pl.ds(j * LANES, LANES)
        fm, cur, bef = row_pack(1, SUBS - 1, j)
        s = speed_coef * jnp.where(sub < 4, pltpu.roll(cur[1], 4, 0), cur[1])
        m = diffuse_coef * jnp.where(sub < 4, pltpu.roll(fm[1], 4, 0), fm[1])
        g = [s * cur[h] + m * bef[h] for h in range(2)]
        for h in range(2):
            puts.append((coef_north, pl.ds(h * SUBS, SUBS), cols, -twice_step * fm[h] * s))
            puts.append((coef_north, pl.ds(ROWS + h * SUBS, SUBS), cols, twice_step * fm[h] * m))
        puts.append((coef_north, pl.ds(2 * ROWS, SUBS), cols, jnp.where(sub < 4, 0.0, -twice_step * gravity * fm[1])))

        fm_s, cur_s, bef_s = row_pack(0, 0, j)
        for h in range(2):
            puts.append((coef_south, pl.ds(h * SUBS, SUBS), cols, twice_step * fm_s[h]))
            puts.append((coef_south, pl.ds(ROWS + h * SUBS, SUBS), cols, twice_step * cur_s[h]))
            puts.append((coef_south, pl.ds(2 * ROWS + h * SUBS, SUBS), cols, -twice_step * bef_s[h]))

        north_going, south_going = g + [s, m], cur_s + bef_s
        for q in range(4):
            puts.append((pay_a, pl.ds(q * SUBS, SUBS), cols, jnp.where(even, north_going[q], south_going[q])))
        into_b.append([jnp.where(even, jnp.where(lat == 0, 0.0, y), x) for x, y in zip(north_going, south_going)])
        turned = [jnp.take_along_axis(x, back, axis=1) for x in cur + bef]
        folded.append([x if q % 2 == 0 else -x for q, x in enumerate(turned)])
    for j in range(n_tiles):
        for q in range(4):
            value = jnp.where(is_top, folded[n_tiles - 1 - j][q], into_b[j][q])
            puts.append((pay_b, pl.ds((4 * j + q) * SUBS, SUBS), slice(None), value))
    for ref, rows, cols, value in puts:
        ref[rows, cols] = value


def inner_kernel(
    total_rows,
    raw_bef, raw_cur, scalar_flags, east_flags, north_flags,
    after_v, filtered_v,
    cur_v, bef_v, pres_v, flux_v,
):
    height, width = raw_cur.shape[2], raw_cur.shape[3]
    n_chunks, n_tiles = height // SUBS, width // LANES
    lat = lax.axis_index("lat")
    flags = (scalar_flags, east_flags, north_flags)

    zero = jnp.zeros((SUBS, LANES), jnp.float32)
    lane = lane_ids((SUBS, LANES))
    sub = row_ids((SUBS, LANES))
    first_lane, last_lane = lane == 0, lane == LANES - 1
    last_sub = sub == SUBS - 1
    tiles = [pl.ds(j * LANES, LANES) for j in range(n_tiles)]
    for l in range(LEVELS):
        for j in range(n_tiles):
            pres_v[l, j, pl.ds(height, SUBS), :] = zero
            for f in range(FIELDS):
                cur_v[f, l, j, pl.ds(height, SUBS), :] = zero
                bef_v[f, l, j, pl.ds(height, SUBS), :] = zero
                flux_v[f, l, j] = zero

    def store(puts):
        for ref, at, value in puts:
            ref[at] = value

    def each(op, *xs):
        return [op(*x) for x in zip(*xs)]

    def east_of(x):
        return [
            pltpu.roll(jnp.where(first_lane, b, a), LANES - 1, 1) for a, b in zip(x, x[1:] + [zero])
        ]

    def west_of(x):
        return [pltpu.roll(jnp.where(last_lane, b, a), 1, 1) for a, b in zip(x, [zero] + x[:-1])]

    def south_of(x, below):
        return [pltpu.roll(jnp.where(last_sub, b, a), 1, 0) for a, b in zip(x, below)]

    def face_flux(s, m, x, x_next, y, y_next):
        return each(lambda s, m, x, xn, y, yn: s * (x + xn) - m * (yn - y), s, m, x, x_next, y, y_next)

    def at(ref, r):
        return [ref[j, r, :] for j in range(n_tiles)]

    half = twice_step

    def unit(c, l, fields):
        rows = pl.ds(pl.multiple_of(c * SUBS, SUBS), SUBS)
        shifted = pl.ds(c * SUBS + 1, SUBS)

        def flag(t):
            return [flags[t][l, rows, cols].astype(jnp.float32) for cols in tiles]

        cur_e = {f: east_of(at(cur_v.at[f, l], rows)) for f in fields}
        bef_e = {f: east_of(at(bef_v.at[f, l], rows)) for f in fields}
        pres_e = east_of(at(pres_v.at[l], rows)) if 2 in fields else None
        yield []
        s_e, m_e = [half * speed_coef * x for x in at(cur_v.at[2, l], rows)], [half * diffuse_coef * x for x in flag(1)]
        s_n, m_n = [half * speed_coef * x for x in at(cur_v.at[3, l], rows)], [half * diffuse_coef * x for x in flag(2)]
        puts, own, west, south = [], {}, {}, {}
        for f in fields:
            cur, bef = at(cur_v.at[f, l], rows), at(bef_v.at[f, l], rows)
            flux_e = face_flux(s_e, m_e, cur, cur_e[f], bef, bef_e[f])
            flux_n = face_flux(s_n, m_n, cur, at(cur_v.at[f, l], shifted), bef, at(bef_v.at[f, l], shifted))
            west[f] = west_of(flux_e)
            south[f] = south_of(flux_n, at(flux_v.at[f, l], slice(None)))
            own[f] = each(lambda e, n: e + n, flux_e, flux_n)
            puts += [(flux_v, (f, l, j), x) for j, x in enumerate(flux_n)]
        yield puts
        puts = []
        for f in fields:
            cur, bef = at(cur_v.at[f, l], rows), at(bef_v.at[f, l], rows)
            mask = flag(mask_of(f))
            tend = each(lambda w, s, o: (w + s) - o, west[f], south[f], own[f])
            if f >= 2:
                index = (lat * height + c * SUBS + sub).astype(jnp.float32)
                cor = half * coriolis * (2.0 * (index + 0.5) / total_rows - 1.0)
                pres = at(pres_v.at[l], rows)
                ahead = pres_e if f == 2 else at(pres_v.at[l], shifted)
                slope = each(lambda m, a, p: (half * gravity) * m * (a - p), mask, ahead, pres)
                if f == 2:
                    tend = each(lambda t, v, g: t + (cor * v - g), tend, at(cur_v.at[3, l], rows), slope)
                else:
                    tend = each(lambda t, u, g: t - (cor * u + g), tend, at(cur_v.at[2, l], rows), slope)
            new = each(lambda b, t, m: (b + t) * m, bef, tend, mask)
            mid = each(lambda c, b, n: (1.0 - 2.0 * asselin) * c + asselin * (b + n), cur, bef, new)
            for cols, a, x in zip(tiles, new, mid):
                puts.append((after_v, (f, l, rows, cols), a))
                puts.append((filtered_v, (f, l, rows, cols), x))
        yield puts

    def masking(c):
        rows = pl.ds(pl.multiple_of(c * SUBS, SUBS), SUBS)
        totals = [zero] * n_tiles
        for l in range(LEVELS):
            for part in (range(0, n_tiles // 2), range(n_tiles // 2, n_tiles)):
                puts = []
                for j in part:
                    cols = tiles[j]
                    masks = [flags[t][l, rows, cols].astype(jnp.float32) for t in range(3)]
                    cur = [raw_cur[f, l, rows, cols] * masks[mask_of(f)] for f in range(FIELDS)]
                    rho = haline * cur[1] - thermal * cur[0]
                    totals[j] = totals[j] + rho
                    puts.append((pres_v, (l, j, rows), totals[j] - 0.5 * rho))
                    for f in range(FIELDS):
                        puts.append((cur_v, (f, l, j, rows), cur[f]))
                        puts.append((bef_v, (f, l, j, rows), raw_bef[f, l, rows, cols] * masks[mask_of(f)]))
                yield puts

    for puts in masking(0):
        store(puts)

    chunks = 4 if n_chunks % 4 == 0 else 1

    def some_chunks(i, carry):
        units = [unit(chunks * i + k, l, range(FIELDS)) for k in range(chunks) for l in range(LEVELS)]
        later = [masking(jnp.minimum(chunks * i + k + 1, n_chunks - 1)) for k in range(chunks)]
        for t in range(len(units) + 2):
            puts = []
            for u in (t, t - 1, t - 2):
                if 0 <= u < len(units):
                    puts += next(units[u])
            if t < len(units):
                puts += next(later[t // LEVELS]) + next(later[t // LEVELS])
            store(puts)
        return carry

    lax.fori_loop(0, n_chunks // chunks, some_chunks, 0)


def rim_kernel(
    got_a, got_b, got_east, got_west, coef_north, coef_south, coef_west, coef_east,
    after_v, filtered_v,
    after, filtered, after_w, filtered_w,
    add_rows, add_cols, sems,
):
    height, width = after.shape[2], after.shape[3]
    n_chunks, n_tiles = height // SUBS, width // LANES
    lane = lane_ids((SUBS, LANES))
    sub = row_ids((SUBS, LANES))
    even = lax.axis_index("lat") % 2 == 0

    def out(i, rows, cols):
        copies = [
            pltpu.make_async_copy(s.at[:, :, rows, cols], d.at[:, :, rows, cols], sems.at[i, q])
            for q, (s, d) in enumerate(((after_w, after), (filtered_w, filtered)))
        ]
        for copy in copies:
            copy.start()
        return copies

    middle = pl.ds(SUBS, height - 2 * SUBS)
    pending = out(2, middle, pl.ds(LANES, width - 2 * LANES))

    for j in range(n_tiles):
        cols = pl.ds(j * LANES, LANES)
        got = [(got_a[pl.ds(q * SUBS, SUBS), cols], got_b[pl.ds((4 * j + q) * SUBS, SUBS), :]) for q in range(4)]
        north = [jnp.where(even, a, b) for a, b in got]
        south = [jnp.where(even, b, a) for a, b in got]

        def coef(ref, q):
            return ref[pl.ds(q * SUBS, SUBS), cols]

        rho = jnp.where(sub < LEVELS, haline * pltpu.roll(north[0], LEVELS, 0) - thermal * north[0], 0.0)
        total = rho + pltpu.roll(rho, 1, 0)
        total = total + pltpu.roll(total, 2, 0)
        pres = pltpu.roll(total - 0.5 * rho, LEVELS, 0)
        for h in range(2):
            at = pl.ds(h * SUBS, SUBS)
            up = coef(coef_north, h) * north[h] + coef(coef_north, 2 + h) * north[2 + h]
            if h == 1:
                up = up + coef(coef_north, 4) * pres
            add_rows[1, at, cols] = up
            add_rows[0, at, cols] = (
                coef(coef_south, h) * south[h]
                + coef(coef_south, 2 + h) * south[2]
                + coef(coef_south, 4 + h) * south[3]
            )

    for side, (got, coef) in enumerate(((got_west[pl.ds(0, height // 2), :], coef_west), (got_east[pl.ds(0, height // 2), :], coef_east))):
        for part in range(2):
            rows = pl.ds(part * (height // 2), height // 2)
            x = got if part == 0 else pltpu.roll(got, LANES // 2, 1)
            x = x * coef[rows, :]
            add_cols[side, rows, :] = (
                x + pltpu.roll(x, LANES - ROWS, 1) + pltpu.roll(x, LANES - 2 * ROWS, 1)
            )

    def edge_cols(rows):
        return add_cols[0, rows, :], add_cols[1, rows, :]

    def put(value, k, at):
        return jnp.where(lane == at, jnp.broadcast_to(value[:, k : k + 1], (SUBS, LANES)), 0.0)

    def apply(extras):
        sums = [(at, after_v[at] + x, filtered_v[at] + asselin * x) for at, x in extras]
        for at, new, mid in sums:
            after_w[at] = new
            filtered_w[at] = mid

    def row_chunk(c, side, line):
        rows = pl.ds(c * SUBS, SUBS)
        west, east = edge_cols(rows)
        for f in range(FIELDS):
            extras = []
            for l in range(LEVELS):
                k = f * LEVELS + l
                for j in range(n_tiles):
                    cols = pl.ds(j * LANES, LANES)
                    extra = jnp.where(sub == line, jnp.broadcast_to(add_rows[side, pl.ds(k, 1), cols], (SUBS, LANES)), 0.0)
                    if j == 0:
                        extra = extra + put(west, k, 0)
                    if j == n_tiles - 1:
                        extra = extra + put(east, k, LANES - 1)
                    extras.append(((f, l, rows, cols), extra))
            apply(extras)

    def side_chunk(c):
        first, last = pl.ds(0, LANES), pl.ds(width - LANES, LANES)
        tiles = [pl.ds(pl.multiple_of(r * SUBS, SUBS), SUBS) for r in (c, c + 1)]
        edges = [edge_cols(rows) for rows in tiles]
        for f in range(FIELDS):
            extras = []
            for l in range(LEVELS):
                k = f * LEVELS + l
                for rows, (west, east) in zip(tiles, edges):
                    extras.append(((f, l, rows, first), put(west, k, 0)))
                    extras.append(((f, l, rows, last), put(east, k, LANES - 1)))
            apply(extras)

    row_chunk(0, 0, 0)
    pending += out(0, pl.ds(0, SUBS), pl.ds(0, width))
    row_chunk(n_chunks - 1, 1, SUBS - 1)
    pending += out(1, pl.ds(height - SUBS, SUBS), pl.ds(0, width))
    for c in range(1, n_chunks - 1, 2):
        side_chunk(c)
        rows = pl.ds(c * SUBS, 2 * SUBS)
        pending += out(2 + c, rows, pl.ds(0, LANES))
        pending += out(3 + c, rows, pl.ds(width - LANES, LANES))
    for copy in pending:
        copy.wait()


def shards(n_lat, earlier_state, present_state, scalar_wet_flags, eastside_wet_flags, northside_wet_flags):
    args = (earlier_state, present_state, scalar_wet_flags, eastside_wet_flags, northside_wet_flags)
    height, width = present_state.shape[2:]
    n_lon = lax.axis_size("lon")
    f32 = jnp.float32
    params = pltpu.CompilerParams(vmem_limit_bytes=VMEM_LIMIT)
    state = (FIELDS, LEVELS, height, width)
    apart = (LEVELS, width // LANES, height + SUBS, LANES)

    wide = 2 * ROWS * (width // LANES)

    def vmem(*shape):
        return pltpu.VMEM(shape, f32)

    edges = pl.pallas_call(
        functools.partial(edges_kernel, n_lat),
        out_shape=[
            vmem(2 * ROWS, width), vmem(wide + 2 * SUBS, LANES),
            vmem(max(wide + SUBS, height // 2), LANES), vmem(max(wide + SUBS, height // 2), LANES),
            vmem(2 * ROWS + SUBS, width), vmem(3 * ROWS, width), vmem(height, LANES), vmem(height, LANES),
        ],
        in_specs=[ANY] * 5,
        out_specs=[VMEM] * 8,
        scratch_shapes=[
            pltpu.VMEM((2, 2, FIELDS, LEVELS, height, LANES), f32),
            pltpu.VMEM((2, 3, LEVELS, height, LANES), jnp.int32),
            pltpu.VMEM((2, 2, FIELDS, LEVELS, SUBS, width), f32),
            pltpu.VMEM((2, 3, LEVELS, SUBS, width), jnp.int32),
            pltpu.SemaphoreType.DMA((20,)),
        ],
        compiler_params=params,
        cost_estimate=pl.CostEstimate(flops=500_000, bytes_accessed=3_600_000, transcendentals=0),
        name="edges",
    )(*[pltpu.with_memory_space_constraint(x, pltpu.HBM) for x in args])
    pay_a, pay_b, pay_west, pay_east, *coefs = edges

    def device(lon, lat):
        return lon * n_lat + lat

    lons, lats, top = range(n_lon), range(n_lat), n_lat - 1
    pairs_a = [(device(lon, lat), device(lon, lat ^ 1)) for lon in lons for lat in lats]
    pairs_b = [
        (
            device(lon, lat),
            device(n_lon - 1 - lon, lat) if lat in (0, top) else device(lon, lat + 1 if lat % 2 else lat - 1),
        )
        for lon in lons
        for lat in lats
    ]
    got_b = lax.ppermute(pay_b, ("lon", "lat"), pairs_b)
    got_a = lax.ppermute(pay_a, ("lon", "lat"), pairs_a)
    got_east = lax.ppermute(pay_west, "lon", [(i, (i - 1) % n_lon) for i in lons])
    got_west = lax.ppermute(pay_east, "lon", [(i, (i + 1) % n_lon) for i in lons])

    after_v, filtered_v = pl.pallas_call(
        functools.partial(inner_kernel, height * n_lat),
        out_shape=[vmem(*state), vmem(*state)],
        in_specs=[VMEM] * 5,
        out_specs=[VMEM, VMEM],
        scratch_shapes=[
            pltpu.VMEM((FIELDS, *apart), f32),
            pltpu.VMEM((FIELDS, *apart), f32),
            pltpu.VMEM(apart, f32),
            pltpu.VMEM((FIELDS, LEVELS, width // LANES, SUBS, LANES), f32),
        ],
        compiler_params=params,
        cost_estimate=pl.CostEstimate(flops=20_000_000, bytes_accessed=9_000_000, transcendentals=0),
        name="inner",
    )(*[pltpu.with_memory_space_constraint(x, pltpu.VMEM) for x in args])

    def in_vmem(x):
        return pltpu.with_memory_space_constraint(x, pltpu.VMEM)

    fixed = [in_vmem(x) for x in (got_a, got_b, got_east, got_west, *coefs, after_v, filtered_v)]
    after, filtered, _, _ = pl.pallas_call(
        rim_kernel,
        out_shape=[pltpu.HBM(state, f32), pltpu.HBM(state, f32), vmem(*state), vmem(*state)],
        in_specs=[VMEM] * 10,
        out_specs=[ANY, ANY, VMEM, VMEM],
        scratch_shapes=[
            pltpu.VMEM((2, ROWS, width), f32),
            pltpu.VMEM((2, height, LANES), f32),
            pltpu.SemaphoreType.DMA((3 + height // SUBS, 2)),
        ],
        input_output_aliases={8: 2, 9: 3},
        compiler_params=params,
        cost_estimate=pl.CostEstimate(flops=500_000, bytes_accessed=3_000_000, transcendentals=0),
        name="rim",
    )(*fixed)
    return after, filtered


def solution(mesh):
    placed = (
        P(None, None, "lat", "lon"),
        P(None, None, "lat", "lon"),
        P(None, "lat", "lon"),
        P(None, "lat", "lon"),
        P(None, "lat", "lon"),
    )
    return jax.shard_map(
        functools.partial(shards, mesh.shape["lat"]),
        mesh=mesh,
        in_specs=placed,
        out_specs=(P(None, None, "lat", "lon"), P(None, None, "lat", "lon")),
        check_vma=False,
    )
```

```python
import functools

import jax
import jax.numpy as jnp
from jax import lax
from jax.experimental import pallas as pl
from jax.experimental.pallas import tpu as pltpu
from jax.sharding import PartitionSpec as P

advect_coef = 0.5
diffuse_coef = 0.25
twice_step = 0.5
gravity = 0.5
coriolis = 0.5
thermal = 0.2
haline = 0.15
asselin = 0.1

LANES = 128
SUBS = 8
FIELDS = 4
LEVELS = 4
ROWS = FIELDS * LEVELS
VMEM_LIMIT = 24 * 1024 * 1024

speed_coef = advect_coef * 0.5
ANY = pl.BlockSpec(memory_space=pl.ANY)
VMEM = pl.BlockSpec(memory_space=pltpu.VMEM)


def mask_of(field):
    return max(field - 1, 0)


def lane_ids(shape):
    return lax.broadcasted_iota(jnp.int32, shape, len(shape) - 1)


def row_ids(shape):
    return lax.broadcasted_iota(jnp.int32, shape, len(shape) - 2)


def edges_kernel(
    n_lat,
    earlier, present, scalar_flags, east_flags, north_flags,
    pay_a, pay_b, pay_west, pay_east, coef_north, coef_south, coef_west, coef_east,
    col_state, col_flag, row_state, row_flag, sems,
):
    height, width = present.shape[2], present.shape[3]
    lat = lax.axis_index("lat")
    flags = (scalar_flags, east_flags, north_flags)
    copies = []
    for side in range(2):
        cols = pl.ds(0 if side == 0 else width - LANES, LANES)
        for t, state in enumerate((present, earlier)):
            copies.append((state.at[:, :, :, cols], col_state.at[side, t]))
        for t, flag in enumerate(flags):
            copies.append((flag.at[:, :, cols], col_flag.at[side, t]))
    for side in range(2):
        rows = pl.ds(0 if side == 0 else height - SUBS, SUBS)
        for t, state in enumerate((present, earlier)):
            copies.append((state.at[:, :, rows, :], row_state.at[side, t]))
        for t, flag in enumerate(flags):
            copies.append((flag.at[:, rows, :], row_flag.at[side, t]))
    copies = [
        pltpu.make_async_copy(src, dst, sems.at[i]) for i, (src, dst) in enumerate(copies)
    ]
    for copy in copies:
        copy.start()
    n_tiles = width // LANES
    lane = lane_ids((SUBS, LANES))
    sub = row_ids((SUBS, LANES))

    for copy in copies[:5]:
        copy.wait()

    base, level = lane & (ROWS - 1), lane & (LEVELS - 1)
    zeros = jnp.zeros((SUBS, LANES), jnp.float32)
    tiles = range(height // SUBS)

    def columns(x, at):
        return [jnp.broadcast_to(x[r * SUBS : (r + 1) * SUBS, at : at + 1], (SUBS, LANES)) for r in tiles]

    def placed(where, xs, old):
        return [jnp.where(where, x, o) for x, o in zip(xs, old)]

    def col_pack(side, at):
        fm, both, extra, u, total = ([zeros] * len(tiles) for _ in range(5))
        for l in range(LEVELS):
            mask = [columns(col_flag[side, t, l].astype(jnp.float32), at) for t in range(3)]
            for f in range(FIELDS):
                fm = placed(base == f * LEVELS + l, mask[mask_of(f)], fm)
            now = []
            for f in range(FIELDS):
                now.append(columns(col_state[side, 0, f, l], at))
                both = placed(lane == f * LEVELS + l, now[f], both)
                both = placed(lane == ROWS + f * LEVELS + l, columns(col_state[side, 1, f, l], at), both)
            if side == 0:
                rho = [(haline * s - thermal * t) * m for s, t, m in zip(now[1], now[0], mask[0])]
                total = [a + b for a, b in zip(total, rho)]
                pres = [a - 0.5 * b for a, b in zip(total, rho)]
                extra = placed(lane == 2 * ROWS + 2 * LEVELS + l, pres, extra)
            else:
                extra = placed(level == l, mask[1], extra)
                u = placed(level == l, now[2], u)
        return zip(fm, both, extra, u)

    in_pres = (lane >= 2 * ROWS + 2 * LEVELS) & (lane < 2 * ROWS + 3 * LEVELS)
    going_west, going_east, coefs_west, coefs_east = [], [], [], []

    def put_column(pay, coef, going, coefs):
        half = len(tiles) // 2
        folded = [jnp.where(lane < LANES // 2, going[r], pltpu.roll(going[r + half], LANES // 2, 1)) for r in range(half)]
        for r in tiles:
            coef[pl.ds(r * SUBS, SUBS), :] = coefs[r]
            if r < half:
                pay[pl.ds(r * SUBS, SUBS), :] = folded[r]

    for fm, both, pres, _ in col_pack(0, 0):
        both = both * fm
        moved = pltpu.roll(both, ROWS, 1)
        going_west.append(both + pres)
        coefs_west.append(twice_step * jnp.where(lane < ROWS, fm, jnp.where(lane < 2 * ROWS, moved, -moved)))
    put_column(pay_west, coef_west, going_west, coefs_west)
    for copy in copies[5:10]:
        copy.wait()
    for fm, both, mu, u in col_pack(1, LANES - 1):
        s, dm = speed_coef * u * mu, diffuse_coef * mu
        own = both * fm * jnp.where(lane < ROWS, s, dm)
        g = own + pltpu.roll(own, LANES - ROWS, 1)
        going_east.append(jnp.where(lane < ROWS, g, jnp.where(lane < 2 * ROWS, s, dm)))
        face = jnp.where(lane < ROWS, -twice_step * s, twice_step * dm) * fm
        coefs_east.append(
            jnp.where(lane < 2 * ROWS, face, jnp.where(in_pres, -twice_step * gravity * mu, 0.0))
        )
    put_column(pay_east, coef_east, going_east, coefs_east)
    for copy in copies[10:]:
        copy.wait()

    def row_pack(side, at, j):
        line = pl.ds(at, 1)
        cols = pl.ds(j * LANES, LANES)

        def gather(rows):
            packed = jnp.broadcast_to(rows[0], (SUBS, LANES))
            for k in range(1, SUBS):
                packed = jnp.where(sub == k, jnp.broadcast_to(rows[k], (SUBS, LANES)), packed)
            return packed

        def flag_row(t, l):
            return row_flag[side, t, l, line, cols].astype(jnp.float32)

        fm = [
            gather([flag_row(mask_of(f), l) for f in (2 * h, 2 * h + 1) for l in range(LEVELS)])
            for h in range(2)
        ]
        cur, bef = (
            [
                fm[h]
                * gather([row_state[side, t, f, l, line, cols] for f in (2 * h, 2 * h + 1) for l in range(LEVELS)])
                for h in range(2)
            ]
            for t in range(2)
        )
        return fm, cur, bef

    back = LANES - 1 - lane
    even = lat % 2 == 0
    is_top = lat == n_lat - 1
    puts = [
        (ref, pl.ds(r, SUBS), slice(None), zeros)
        for ref, used in ((pay_b, 2 * ROWS * n_tiles), (pay_west, height // 2), (pay_east, height // 2))
        for r in range(used, ref.shape[0], SUBS)
    ]
    into_b, folded = [], []
    for j in range(n_tiles):
        cols = pl.ds(j * LANES, LANES)
        fm, cur, bef = row_pack(1, SUBS - 1, j)
        s = speed_coef * jnp.where(sub < 4, pltpu.roll(cur[1], 4, 0), cur[1])
        m = diffuse_coef * jnp.where(sub < 4, pltpu.roll(fm[1], 4, 0), fm[1])
        g = [s * cur[h] + m * bef[h] for h in range(2)]
        for h in range(2):
            puts.append((coef_north, pl.ds(h * SUBS, SUBS), cols, -twice_step * fm[h] * s))
            puts.append((coef_north, pl.ds(ROWS + h * SUBS, SUBS), cols, twice_step * fm[h] * m))
        puts.append((coef_north, pl.ds(2 * ROWS, SUBS), cols, jnp.where(sub < 4, 0.0, -twice_step * gravity * fm[1])))

        fm_s, cur_s, bef_s = row_pack(0, 0, j)
        for h in range(2):
            puts.append((coef_south, pl.ds(h * SUBS, SUBS), cols, twice_step * fm_s[h]))
            puts.append((coef_south, pl.ds(ROWS + h * SUBS, SUBS), cols, twice_step * cur_s[h]))
            puts.append((coef_south, pl.ds(2 * ROWS + h * SUBS, SUBS), cols, -twice_step * bef_s[h]))

        north_going, south_going = g + [s, m], cur_s + bef_s
        for q in range(4):
            puts.append((pay_a, pl.ds(q * SUBS, SUBS), cols, jnp.where(even, north_going[q], south_going[q])))
        into_b.append([jnp.where(even, jnp.where(lat == 0, 0.0, y), x) for x, y in zip(north_going, south_going)])
        turned = [jnp.take_along_axis(x, back, axis=1) for x in cur + bef]
        folded.append([x if q % 2 == 0 else -x for q, x in enumerate(turned)])
    for j in range(n_tiles):
        for q in range(4):
            value = jnp.where(is_top, folded[n_tiles - 1 - j][q], into_b[j][q])
            puts.append((pay_b, pl.ds((4 * j + q) * SUBS, SUBS), slice(None), value))
    for ref, rows, cols, value in puts:
        ref[rows, cols] = value


def inner_kernel(
    total_rows,
    raw_bef, raw_cur, scalar_flags, east_flags, north_flags,
    after_v, filtered_v,
    cur_v, bef_v, pres_v, flux_v,
):
    height, width = raw_cur.shape[2], raw_cur.shape[3]
    n_chunks, n_tiles = height // SUBS, width // LANES
    lat = lax.axis_index("lat")
    flags = (scalar_flags, east_flags, north_flags)

    zero = jnp.zeros((SUBS, LANES), jnp.float32)
    lane = lane_ids((SUBS, LANES))
    sub = row_ids((SUBS, LANES))
    first_lane, last_lane = lane == 0, lane == LANES - 1
    last_sub = sub == SUBS - 1
    tiles = [pl.ds(j * LANES, LANES) for j in range(n_tiles)]
    for l in range(LEVELS):
        for j in range(n_tiles):
            pres_v[l, j, pl.ds(height, SUBS), :] = zero
            for f in range(FIELDS):
                cur_v[f, l, j, pl.ds(height, SUBS), :] = zero
                bef_v[f, l, j, pl.ds(height, SUBS), :] = zero
                flux_v[f, l, j] = zero

    def store(puts):
        for ref, at, value in puts:
            ref[at] = value

    def each(op, *xs):
        return [op(*x) for x in zip(*xs)]

    def east_of(x):
        return [
            pltpu.roll(jnp.where(first_lane, b, a), LANES - 1, 1) for a, b in zip(x, x[1:] + [zero])
        ]

    def west_of(x):
        return [pltpu.roll(jnp.where(last_lane, b, a), 1, 1) for a, b in zip(x, [zero] + x[:-1])]

    def south_of(x, below):
        return [pltpu.roll(jnp.where(last_sub, b, a), 1, 0) for a, b in zip(x, below)]

    def face_flux(s, m, x, x_next, y, y_next):
        return each(lambda s, m, x, xn, y, yn: s * (x + xn) - m * (yn - y), s, m, x, x_next, y, y_next)

    def at(ref, r):
        return [ref[j, r, :] for j in range(n_tiles)]

    half = twice_step

    def unit(c, l, fields):
        rows = pl.ds(pl.multiple_of(c * SUBS, SUBS), SUBS)
        shifted = pl.ds(c * SUBS + 1, SUBS)

        def flag(t):
            return [flags[t][l, rows, cols].astype(jnp.float32) for cols in tiles]

        cur_e = {f: east_of(at(cur_v.at[f, l], rows)) for f in fields}
        bef_e = {f: east_of(at(bef_v.at[f, l], rows)) for f in fields}
        pres_e = east_of(at(pres_v.at[l], rows)) if 2 in fields else None
        yield []
        s_e, m_e = [half * speed_coef * x for x in at(cur_v.at[2, l], rows)], [half * diffuse_coef * x for x in flag(1)]
        s_n, m_n = [half * speed_coef * x for x in at(cur_v.at[3, l], rows)], [half * diffuse_coef * x for x in flag(2)]
        puts, own, west, south = [], {}, {}, {}
        for f in fields:
            cur, bef = at(cur_v.at[f, l], rows), at(bef_v.at[f, l], rows)
            flux_e = face_flux(s_e, m_e, cur, cur_e[f], bef, bef_e[f])
            flux_n = face_flux(s_n, m_n, cur, at(cur_v.at[f, l], shifted), bef, at(bef_v.at[f, l], shifted))
            west[f] = west_of(flux_e)
            south[f] = south_of(flux_n, at(flux_v.at[f, l], slice(None)))
            own[f] = each(lambda e, n: e + n, flux_e, flux_n)
            puts += [(flux_v, (f, l, j), x) for j, x in enumerate(flux_n)]
        yield puts
        puts = []
        for f in fields:
            cur, bef = at(cur_v.at[f, l], rows), at(bef_v.at[f, l], rows)
            mask = flag(mask_of(f))
            tend = each(lambda w, s, o: (w + s) - o, west[f], south[f], own[f])
            if f >= 2:
                index = (lat * height + c * SUBS + sub).astype(jnp.float32)
                cor = half * coriolis * (2.0 * (index + 0.5) / total_rows - 1.0)
                pres = at(pres_v.at[l], rows)
                ahead = pres_e if f == 2 else at(pres_v.at[l], shifted)
                slope = each(lambda m, a, p: (half * gravity) * m * (a - p), mask, ahead, pres)
                if f == 2:
                    tend = each(lambda t, v, g: t + (cor * v - g), tend, at(cur_v.at[3, l], rows), slope)
                else:
                    tend = each(lambda t, u, g: t - (cor * u + g), tend, at(cur_v.at[2, l], rows), slope)
            new = each(lambda b, t, m: (b + t) * m, bef, tend, mask)
            mid = each(lambda c, b, n: (1.0 - 2.0 * asselin) * c + asselin * (b + n), cur, bef, new)
            for cols, a, x in zip(tiles, new, mid):
                puts.append((after_v, (f, l, rows, cols), a))
                puts.append((filtered_v, (f, l, rows, cols), x))
        yield puts

    def masking(c):
        rows = pl.ds(pl.multiple_of(c * SUBS, SUBS), SUBS)
        totals = [zero] * n_tiles
        for l in range(LEVELS):
            for part in (range(0, n_tiles // 2), range(n_tiles // 2, n_tiles)):
                puts = []
                for j in part:
                    cols = tiles[j]
                    masks = [flags[t][l, rows, cols].astype(jnp.float32) for t in range(3)]
                    cur = [raw_cur[f, l, rows, cols] * masks[mask_of(f)] for f in range(FIELDS)]
                    rho = haline * cur[1] - thermal * cur[0]
                    totals[j] = totals[j] + rho
                    puts.append((pres_v, (l, j, rows), totals[j] - 0.5 * rho))
                    for f in range(FIELDS):
                        puts.append((cur_v, (f, l, j, rows), cur[f]))
                        puts.append((bef_v, (f, l, j, rows), raw_bef[f, l, rows, cols] * masks[mask_of(f)]))
                yield puts

    for puts in masking(0):
        store(puts)

    chunks = next(k for k in (8, 4, 2, 1) if n_chunks % k == 0)

    def some_chunks(i, carry):
        units = [unit(chunks * i + k, l, range(FIELDS)) for k in range(chunks) for l in range(LEVELS)]
        later = [masking(jnp.minimum(chunks * i + k + 1, n_chunks - 1)) for k in range(chunks)]
        for t in range(len(units) + 2):
            puts = []
            for u in (t, t - 1, t - 2):
                if 0 <= u < len(units):
                    puts += next(units[u])
            if t < len(units):
                puts += next(later[t // LEVELS]) + next(later[t // LEVELS])
            store(puts)
        return carry

    lax.fori_loop(0, n_chunks // chunks, some_chunks, 0)


def rim_kernel(
    got_a, got_b, got_east, got_west, coef_north, coef_south, coef_west, coef_east,
    after_v, filtered_v,
    after, filtered, after_w, filtered_w,
    add_rows, add_cols, sems,
):
    height, width = after.shape[2], after.shape[3]
    n_chunks, n_tiles = height // SUBS, width // LANES
    lane = lane_ids((SUBS, LANES))
    sub = row_ids((SUBS, LANES))
    even = lax.axis_index("lat") % 2 == 0

    def out(i, rows, cols):
        copies = [
            pltpu.make_async_copy(s.at[:, :, rows, cols], d.at[:, :, rows, cols], sems.at[i, q])
            for q, (s, d) in enumerate(((after_w, after), (filtered_w, filtered)))
        ]
        for copy in copies:
            copy.start()
        return copies

    middle = pl.ds(SUBS, height - 2 * SUBS)
    pending = out(2, middle, pl.ds(LANES, width - 2 * LANES))

    for j in range(n_tiles):
        cols = pl.ds(j * LANES, LANES)
        got = [(got_a[pl.ds(q * SUBS, SUBS), cols], got_b[pl.ds((4 * j + q) * SUBS, SUBS), :]) for q in range(4)]
        north = [jnp.where(even, a, b) for a, b in got]
        south = [jnp.where(even, b, a) for a, b in got]

        def coef(ref, q):
            return ref[pl.ds(q * SUBS, SUBS), cols]

        rho = jnp.where(sub < LEVELS, haline * pltpu.roll(north[0], LEVELS, 0) - thermal * north[0], 0.0)
        total = rho + pltpu.roll(rho, 1, 0)
        total = total + pltpu.roll(total, 2, 0)
        pres = pltpu.roll(total - 0.5 * rho, LEVELS, 0)
        for h in range(2):
            at = pl.ds(h * SUBS, SUBS)
            up = coef(coef_north, h) * north[h] + coef(coef_north, 2 + h) * north[2 + h]
            if h == 1:
                up = up + coef(coef_north, 4) * pres
            add_rows[1, at, cols] = up
            add_rows[0, at, cols] = (
                coef(coef_south, h) * south[h]
                + coef(coef_south, 2 + h) * south[2]
                + coef(coef_south, 4 + h) * south[3]
            )

    for side, (got, coef) in enumerate(((got_west[pl.ds(0, height // 2), :], coef_west), (got_east[pl.ds(0, height // 2), :], coef_east))):
        for part in range(2):
            rows = pl.ds(part * (height // 2), height // 2)
            x = got if part == 0 else pltpu.roll(got, LANES // 2, 1)
            x = x * coef[rows, :]
            add_cols[side, rows, :] = (
                x + pltpu.roll(x, LANES - ROWS, 1) + pltpu.roll(x, LANES - 2 * ROWS, 1)
            )

    def edge_cols(rows):
        return add_cols[0, rows, :], add_cols[1, rows, :]

    def put(value, k, at):
        return jnp.where(lane == at, jnp.broadcast_to(value[:, k : k + 1], (SUBS, LANES)), 0.0)

    def apply(extras):
        sums = [(at, after_v[at] + x, filtered_v[at] + asselin * x) for at, x in extras]
        for at, new, mid in sums:
            after_w[at] = new
            filtered_w[at] = mid

    def row_chunk(c, side, line):
        rows = pl.ds(c * SUBS, SUBS)
        west, east = edge_cols(rows)
        for f in range(FIELDS):
            extras = []
            for l in range(LEVELS):
                k = f * LEVELS + l
                for j in range(n_tiles):
                    cols = pl.ds(j * LANES, LANES)
                    extra = jnp.where(sub == line, jnp.broadcast_to(add_rows[side, pl.ds(k, 1), cols], (SUBS, LANES)), 0.0)
                    if j == 0:
                        extra = extra + put(west, k, 0)
                    if j == n_tiles - 1:
                        extra = extra + put(east, k, LANES - 1)
                    extras.append(((f, l, rows, cols), extra))
            apply(extras)

    def side_chunk(c):
        first, last = pl.ds(0, LANES), pl.ds(width - LANES, LANES)
        tiles = [pl.ds(pl.multiple_of(r * SUBS, SUBS), SUBS) for r in (c, c + 1)]
        edges = [edge_cols(rows) for rows in tiles]
        for f in range(FIELDS):
            extras = []
            for l in range(LEVELS):
                k = f * LEVELS + l
                for rows, (west, east) in zip(tiles, edges):
                    extras.append(((f, l, rows, first), put(west, k, 0)))
                    extras.append(((f, l, rows, last), put(east, k, LANES - 1)))
            apply(extras)

    row_chunk(0, 0, 0)
    pending += out(0, pl.ds(0, SUBS), pl.ds(0, width))
    row_chunk(n_chunks - 1, 1, SUBS - 1)
    pending += out(1, pl.ds(height - SUBS, SUBS), pl.ds(0, width))
    for c in range(1, n_chunks - 1, 2):
        side_chunk(c)
        rows = pl.ds(c * SUBS, 2 * SUBS)
        pending += out(2 + c, rows, pl.ds(0, LANES))
        pending += out(3 + c, rows, pl.ds(width - LANES, LANES))
    for copy in pending:
        copy.wait()


def shards(n_lat, earlier_state, present_state, scalar_wet_flags, eastside_wet_flags, northside_wet_flags):
    args = (earlier_state, present_state, scalar_wet_flags, eastside_wet_flags, northside_wet_flags)
    height, width = present_state.shape[2:]
    n_lon = lax.axis_size("lon")
    f32 = jnp.float32
    params = pltpu.CompilerParams(vmem_limit_bytes=VMEM_LIMIT)
    state = (FIELDS, LEVELS, height, width)
    apart = (LEVELS, width // LANES, height + SUBS, LANES)

    wide = 2 * ROWS * (width // LANES)

    def vmem(*shape):
        return pltpu.VMEM(shape, f32)

    edges = pl.pallas_call(
        functools.partial(edges_kernel, n_lat),
        out_shape=[
            vmem(2 * ROWS, width), vmem(wide + 2 * SUBS, LANES),
            vmem(max(wide + SUBS, height // 2), LANES), vmem(max(wide + SUBS, height // 2), LANES),
            vmem(2 * ROWS + SUBS, width), vmem(3 * ROWS, width), vmem(height, LANES), vmem(height, LANES),
        ],
        in_specs=[ANY] * 5,
        out_specs=[VMEM] * 8,
        scratch_shapes=[
            pltpu.VMEM((2, 2, FIELDS, LEVELS, height, LANES), f32),
            pltpu.VMEM((2, 3, LEVELS, height, LANES), jnp.int32),
            pltpu.VMEM((2, 2, FIELDS, LEVELS, SUBS, width), f32),
            pltpu.VMEM((2, 3, LEVELS, SUBS, width), jnp.int32),
            pltpu.SemaphoreType.DMA((20,)),
        ],
        compiler_params=params,
        cost_estimate=pl.CostEstimate(flops=500_000, bytes_accessed=3_600_000, transcendentals=0),
        name="edges",
    )(*[pltpu.with_memory_space_constraint(x, pltpu.HBM) for x in args])
    pay_a, pay_b, pay_west, pay_east, *coefs = edges

    def device(lon, lat):
        return lon * n_lat + lat

    lons, lats, top = range(n_lon), range(n_lat), n_lat - 1
    pairs_a = [(device(lon, lat), device(lon, lat ^ 1)) for lon in lons for lat in lats]
    pairs_b = [
        (
            device(lon, lat),
            device(n_lon - 1 - lon, lat) if lat in (0, top) else device(lon, lat + 1 if lat % 2 else lat - 1),
        )
        for lon in lons
        for lat in lats
    ]
    got_b = lax.ppermute(pay_b, ("lon", "lat"), pairs_b)
    got_a = lax.ppermute(pay_a, ("lon", "lat"), pairs_a)
    got_east = lax.ppermute(pay_west, "lon", [(i, (i - 1) % n_lon) for i in lons])
    got_west = lax.ppermute(pay_east, "lon", [(i, (i + 1) % n_lon) for i in lons])

    after_v, filtered_v = pl.pallas_call(
        functools.partial(inner_kernel, height * n_lat),
        out_shape=[vmem(*state), vmem(*state)],
        in_specs=[VMEM] * 5,
        out_specs=[VMEM, VMEM],
        scratch_shapes=[
            pltpu.VMEM((FIELDS, *apart), f32),
            pltpu.VMEM((FIELDS, *apart), f32),
            pltpu.VMEM(apart, f32),
            pltpu.VMEM((FIELDS, LEVELS, width // LANES, SUBS, LANES), f32),
        ],
        compiler_params=params,
        cost_estimate=pl.CostEstimate(flops=20_000_000, bytes_accessed=9_000_000, transcendentals=0),
        name="inner",
    )(*[pltpu.with_memory_space_constraint(x, pltpu.VMEM) for x in args])

    def in_vmem(x):
        return pltpu.with_memory_space_constraint(x, pltpu.VMEM)

    fixed = [in_vmem(x) for x in (got_a, got_b, got_east, got_west, *coefs, after_v, filtered_v)]
    after, filtered, _, _ = pl.pallas_call(
        rim_kernel,
        out_shape=[pltpu.HBM(state, f32), pltpu.HBM(state, f32), vmem(*state), vmem(*state)],
        in_specs=[VMEM] * 10,
        out_specs=[ANY, ANY, VMEM, VMEM],
        scratch_shapes=[
            pltpu.VMEM((2, ROWS, width), f32),
            pltpu.VMEM((2, height, LANES), f32),
            pltpu.SemaphoreType.DMA((3 + height // SUBS, 2)),
        ],
        input_output_aliases={8: 2, 9: 3},
        compiler_params=params,
        cost_estimate=pl.CostEstimate(flops=500_000, bytes_accessed=3_000_000, transcendentals=0),
        name="rim",
    )(*fixed)
    return after, filtered


def solution(mesh):
    placed = (
        P(None, None, "lat", "lon"),
        P(None, None, "lat", "lon"),
        P(None, "lat", "lon"),
        P(None, "lat", "lon"),
        P(None, "lat", "lon"),
    )
    return jax.shard_map(
        functools.partial(shards, mesh.shape["lat"]),
        mesh=mesh,
        in_specs=placed,
        out_specs=(P(None, None, "lat", "lon"), P(None, None, "lat", "lon")),
        check_vma=False,
    )
```
